128 devices in a mesh: dp: 4 (over y_hi, core), seq: 32 (over z, y_lo, x).
Axes of the slice: x: 4, y: 4 (y_hi: 2, y_lo: 2; y = y_hi * 2 + y_lo), z: 4, core: 2. Of those that a mesh axis runs over, the one named last changes fastest.
Arguments:
- query: bfloat16 [4, 8192, 1152], P('dp', 'seq'), may hold values from -14 to 14
- key: bfloat16 [4, 8192, 1152], P('dp', 'seq'), may hold values from -14 to 14
- value: bfloat16 [4, 8192, 1152], P('dp', 'seq'), may hold values from -6 to 6
- grad_out: bfloat16 [4, 8192, 1152], P('dp', 'seq'), may hold values from -6 to 6
- out_proj: bfloat16 [1152, 1152], replicated, may hold values from -0.1875 to 0.1875
- lengths: int32 [4, 32], P('dp'), may hold values from 1 to 512, 8192 in all within a row
Outputs:
- grad_query: bfloat16 [4, 8192, 1152], P('dp', 'seq')
- grad_key: bfloat16 [4, 8192, 1152], P('dp', 'seq')
- grad_value: bfloat16 [4, 8192, 1152], P('dp', 'seq')
- grad_proj: float32 [1152, 1152], P('seq')
The draws below stay inside these ranges and needn't reach their ends.
All inputs are finite; a program needn't handle non-finite values.
Results may differ from the reference program's by a relative error of at most 0.025.
Values may be sent and summed in bfloat16 or wider, within the bound.
No kernel may reach another device: no remote copies, remote signals or barrier semaphores. Data moves between devices by JAX's collectives and lax.ppermute only.
A program may use at most 128 MiB of HBM per device.

```python
import math
import jax
import jax.numpy as jnp
import numpy as np
from jax import lax

D = 1152
HEADS = 16
HEAD_DIM = 72
TOK_DEV = 256
SPAN = 2
LMAX = 512
PACKS = 4
TOKENS = 8192
IMAGES = 32


def draw_query(key, part):
    key = jax.random.fold_in(key, 101)
    values = jnp.clip(jax.random.normal(key, (PACKS, TOKENS, D), jnp.float32), -4.0, 4.0)
    return values.astype(jnp.bfloat16)


def draw_key(key, part):
    key = jax.random.fold_in(key, 202)
    values = jnp.clip(jax.random.normal(key, (PACKS, TOKENS, D), jnp.float32), -4.0, 4.0)
    return values.astype(jnp.bfloat16)


def with_spikes(entries, stream_key, source, target, parts, factor):
    def block_of(axis_at):
        return (jnp.arange(entries.shape[axis_at]) // (entries.shape[axis_at] // parts)).reshape((-1,) + (1,) * (entries.ndim - 1 - axis_at))

    one_side = jax.random.permutation(stream_key, parts)[block_of(target)]
    other_side = (block_of(target) + parts // 2) % parts
    return jnp.where((block_of(source) == one_side) | (block_of(source) == other_side), factor * entries, entries)


def shard_levels(rng, extent, cuts, smallest, top_value):
    gain = 1.0
    for axis_at, shards_of in cuts:
        heights = jax.random.uniform(jax.random.fold_in(jax.random.fold_in(rng, 6), axis_at), (shards_of,), jnp.float32, smallest / len(cuts), top_value / len(cuts))
        gain = gain * jnp.repeat(jnp.exp(heights), extent[axis_at] // shards_of).reshape((-1,) + (1,) * (len(extent) - 1 - axis_at))
    return gain


def length_profile(count, total, bound, skew):
    weights = [(1 << 20) // math.isqrt(standing ** skew) + 1 for standing in range(2, count + 1)]
    surplus, given = total - bound - (count - 1), [1] * (count - 1)
    while surplus > 0:
        movable = [i for i in range(count - 1) if given[i] < bound]
        pool, remaining = sum([weights[i] for i in movable]), surplus
        for i in movable:
            addition = min(bound - given[i], max(1, remaining * weights[i] // pool), surplus)
            given[i] = given[i] + addition
            surplus = surplus - addition
    return np.array([bound] + given)


def uneven(stream_key, count, total, reach, slope):
    if count == 2:
        one = jax.random.randint(stream_key, (), max(1, total - reach), min(reach, total - 1) + 1)
        return jnp.stack([one, total - one])
    tallies = jnp.asarray(length_profile(count, total, reach, slope), jnp.int32)
    pairs = (count - 1) // 2
    giver, taker = tallies[1:1 + 2 * pairs:2], tallies[2:2 + 2 * pairs:2]
    room = jnp.minimum(giver - 1, reach - taker)
    shifted = jax.random.randint(jax.random.fold_in(stream_key, 1), (pairs,), 0, 1 << 20) % (room + 1)
    tallies = tallies.at[1:1 + 2 * pairs:2].set(giver - shifted).at[2:2 + 2 * pairs:2].set(taker + shifted)
    return tallies[jax.random.permutation(jax.random.fold_in(stream_key, 2), count)]


def bell_draw(key, extent, deviation, most, shards=(), kind=jnp.bfloat16):
    gain = shard_levels(key, extent, shards, -0.22, 0.18) if shards else 1.0
    entries = jax.random.normal(key, extent, jnp.float32) * deviation * gain
    return jnp.minimum(jnp.maximum(entries, -most), most).astype(kind)


def bell_draw_with(key, dims, scale, bound, pieces, heavy, held_as=jnp.bfloat16):
    drawn = scale * jax.random.normal(key, dims, jnp.float32)
    if pieces:
        drawn = drawn * shard_levels(key, dims, pieces, -0.22, 0.18)
    return jnp.clip(with_spikes(drawn, jax.random.fold_in(key, 3), *heavy), -bound, bound).astype(held_as)


def setup_inputs(seed: int = 0) -> dict:
    keys = jax.random.split(jax.random.key(seed), 7)
    query = draw_query(jax.random.fold_in(keys[6], 71), 0)
    key = draw_key(jax.random.fold_in(keys[6], 71), 0)
    value = bell_draw(keys[2], (PACKS, TOKENS, D), 1.0, 6.0, ((0, 4), (1, 32)))
    grad_out = bell_draw_with(keys[3], (PACKS, TOKENS, D), 1.0, 6.0, ((0, 4), (1, 32)), (1, 2, 32, 2.75))
    out_proj = bell_draw(keys[4], (D, D), D ** -0.5, 0.1875)
    lengths = jax.vmap(lambda own: uneven(own, IMAGES, TOKENS, LMAX, 2))(jax.random.split(keys[5], PACKS)).reshape((PACKS, IMAGES)).astype(jnp.int32)
    return dict(query=query, key=key, value=value, grad_out=grad_out, out_proj=out_proj, lengths=lengths)


def head_view(array):
    return array.astype(jnp.float32).reshape(array.shape[0], HEADS, HEAD_DIM)


def image_ids(lengths, positions):
    image_ends = jnp.cumsum(lengths).astype(jnp.int32)
    found = jnp.sum((image_ends[None, :] <= positions[:, None]).astype(jnp.int32), axis=1).astype(jnp.int32)
    inside = (positions >= 0) & (positions < TOKENS)
    return jnp.where(inside, found, -1).astype(jnp.int32)


def tile_scores(q_heads, q_ids, k_heads, k_ids):
    scores = jnp.einsum("qhd,khd->hqk", q_heads, k_heads) * (HEAD_DIM ** -0.5)
    allowed = (q_ids[:, None] == k_ids[None, :])[None, :, :]
    return scores, allowed


def tile_grads(q_heads, q_ids, do_heads, log_block, dots_block, k_heads, v_heads, k_ids):
    scores, allowed = tile_scores(q_heads, q_ids, k_heads, k_ids)
    weights = jnp.where(allowed, jnp.exp(scores - log_block[:, :, None]), 0.0)
    dprob = jnp.einsum("qhd,khd->hqk", do_heads, v_heads)
    dscore = (weights * (dprob - dots_block[:, :, None]) * (HEAD_DIM ** -0.5)).astype(jnp.bfloat16)
    return weights.astype(jnp.bfloat16), dscore


def rows_of(array, start, count):
    return lax.dynamic_slice_in_dim(array, start, count, 0)


def one_pack(query, key, value, grad_out, out_proj, lengths):
    margin = SPAN * TOK_DEV
    window = TOK_DEV + 2 * margin
    own_ids = image_ids(lengths, jnp.arange(TOKENS, dtype=jnp.int32))
    padded_ids = image_ids(lengths, jnp.arange(-margin, TOKENS + margin, dtype=jnp.int32))

    def padded(array):
        return jnp.pad(array, ((margin, margin), (0, 0)))

    key_pad = padded(key)
    value_pad = padded(value)
    starts = jnp.arange(TOKENS // TOK_DEV, dtype=jnp.int32) * TOK_DEV

    def log_totals(start):
        scores, allowed = tile_scores(head_view(rows_of(query, start, TOK_DEV)), rows_of(own_ids, start, TOK_DEV),
                                      head_view(rows_of(key_pad, start, window)), rows_of(padded_ids, start, window))
        row_top = jnp.max(jnp.where(allowed, scores, -jnp.inf), axis=2)
        summed = jnp.sum(jnp.where(allowed, jnp.exp(scores - row_top[:, :, None]), 0.0), axis=2)
        return jnp.transpose(row_top + jnp.log(summed))

    log_rows = lax.map(log_totals, starts).reshape(TOKENS, HEADS)

    def attend(start):
        scores, allowed = tile_scores(head_view(rows_of(query, start, TOK_DEV)), rows_of(own_ids, start, TOK_DEV),
                                      head_view(rows_of(key_pad, start, window)), rows_of(padded_ids, start, window))
        log_block = jnp.transpose(rows_of(log_rows, start, TOK_DEV))
        probs = jnp.where(allowed, jnp.exp(scores - log_block[:, :, None]), 0.0).astype(jnp.bfloat16)
        mixed = jnp.einsum("hqk,khd->qhd", probs.astype(jnp.float32), head_view(rows_of(value_pad, start, window)))
        return mixed.reshape(TOK_DEV, D).astype(jnp.bfloat16)

    attn = lax.map(attend, starts).reshape(TOKENS, D)
    d_attn = jnp.dot(grad_out, out_proj, preferred_element_type=jnp.float32).astype(jnp.bfloat16)
    row_dots = jnp.sum(head_view(d_attn) * head_view(attn), axis=2)
    weight_part = jnp.dot(jnp.transpose(grad_out), attn, preferred_element_type=jnp.float32)

    def query_side(start):
        k_heads = head_view(rows_of(key_pad, start, window))
        probs, dscore = tile_grads(head_view(rows_of(query, start, TOK_DEV)), rows_of(own_ids, start, TOK_DEV),
                                   head_view(rows_of(d_attn, start, TOK_DEV)),
                                   jnp.transpose(rows_of(log_rows, start, TOK_DEV)),
                                   jnp.transpose(rows_of(row_dots, start, TOK_DEV)),
                                   k_heads, head_view(rows_of(value_pad, start, window)), rows_of(padded_ids, start, window))
        grad_q = jnp.einsum("hqk,khd->qhd", dscore.astype(jnp.float32), k_heads)
        return grad_q.reshape(TOK_DEV, D).astype(jnp.bfloat16)

    grad_query = lax.map(query_side, starts).reshape(TOKENS, D)
    query_pad = padded(query)
    dattn_pad = padded(d_attn)
    log_pad = padded(log_rows)
    dots_pad = padded(row_dots)

    def key_side(start):
        q_heads = head_view(rows_of(query_pad, start, window))
        do_heads = head_view(rows_of(dattn_pad, start, window))
        probs, dscore = tile_grads(q_heads, rows_of(padded_ids, start, window), do_heads,
                                   jnp.transpose(rows_of(log_pad, start, window)),
                                   jnp.transpose(rows_of(dots_pad, start, window)),
                                   head_view(rows_of(key, start, TOK_DEV)), head_view(rows_of(value, start, TOK_DEV)),
                                   rows_of(own_ids, start, TOK_DEV))
        grad_k = jnp.einsum("hqk,qhd->khd", dscore.astype(jnp.float32), q_heads)
        grad_v = jnp.einsum("hqk,qhd->khd", probs.astype(jnp.float32), do_heads)
        return (grad_k.reshape(TOK_DEV, D).astype(jnp.bfloat16), grad_v.reshape(TOK_DEV, D).astype(jnp.bfloat16))

    grad_k_blocks, grad_v_blocks = lax.map(key_side, starts)
    return grad_query, grad_k_blocks.reshape(TOKENS, D), grad_v_blocks.reshape(TOKENS, D), weight_part


def reference(query, key, value, grad_out, out_proj, lengths):
    query_list, key_list, value_list = [], [], []
    grad_proj = jnp.zeros((D, D), jnp.float32)
    for pack in range(PACKS):
        grad_q, grad_k, grad_v, weight_part = one_pack(query[pack], key[pack], value[pack], grad_out[pack], out_proj, lengths[pack])
        query_list.append(grad_q)
        key_list.append(grad_k)
        value_list.append(grad_v)
        grad_proj = grad_proj + weight_part
    return jnp.stack(query_list), jnp.stack(key_list), jnp.stack(value_list), grad_proj
```

```python
import functools
import jax
import jax.numpy as jnp
from jax import lax
from jax.experimental import pallas as pl
from jax.experimental.pallas import tpu as pltpu
from jax.sharding import PartitionSpec as P

HEADS = 16
HEAD_DIM = 72
ROWS = 256
WIDTH = 1152
WINDOW = 512
REACH = 3 * ROWS
PARTS = 2
PART = WIDTH // PARTS
PART_HEADS = HEADS // PARTS
IMAGES = 32
SCALE = HEAD_DIM ** (-0.5)
LOG2E = 1.4426950408889634
FAR = 1e30
BF16 = jnp.bfloat16
F32 = jnp.float32
VMEM_LIMIT = 56 * 1024 * 1024

NN = (((1,), (0,)), ((), ()))
NT = (((1,), (1,)), ((), ()))
TN = (((0,), (0,)), ((), ()))


def dot(a, b, dims):
    return lax.dot_general(a, b, dims, preferred_element_type=F32)


def call(kernel, out_shape, in_specs, scratch, flops, **more):
    whole = pl.BlockSpec(memory_space=pltpu.VMEM)
    return pl.pallas_call(
        kernel,
        out_shape=out_shape,
        in_specs=[whole if s is None else s for s in in_specs],
        out_specs=jax.tree.map(lambda _: whole, out_shape),
        scratch_shapes=scratch,
        compiler_params=pltpu.CompilerParams(vmem_limit_bytes=VMEM_LIMIT),
        cost_estimate=pl.CostEstimate(flops=flops, bytes_accessed=8 << 20, transcendentals=0),
        **more,
    )


def turn_kernel(q_ref, k_ref, v_ref, *out_refs):
    for at, ref in enumerate((q_ref, k_ref, v_ref)):
        turned = jnp.transpose(ref[...])
        for part in range(PARTS):
            out_refs[part][at * PART : (at + 1) * PART, :] = turned[part * PART : (part + 1) * PART]


def turn(q, k, v):
    shape = jax.ShapeDtypeStruct((3 * PART, ROWS), BF16)
    return call(turn_kernel, (shape,) * PARTS, [None] * 3, [], 1 << 20)(q, k, v)


def attend_kernel(
    place_ref, length_ref, qkv_l, qkv_c, qkv_r, go_l, go_c, go_r, proj_ref,
    attn_ref, back_l, back_c, back_r,
    held, d_attn, result, member, bias,
):
    mine = place_ref[0]
    first = (mine - 1) * ROWS

    def scan(i, carry):
        start, low = carry
        end = start + length_ref[0, i]
        owned = (start + end) // 2 // ROWS == mine
        low = jnp.where(owned, jnp.minimum(low, start - first), low)
        return end, low

    _, low = lax.fori_loop(0, IMAGES, scan, (jnp.int32(0), jnp.int32(REACH - WINDOW)))
    positions = first + low + lax.broadcasted_iota(jnp.int32, (1, WINDOW), 1)

    def mark(i, start):
        end = start + length_ref[0, i]
        owned = (start + end) // 2 // ROWS == mine
        inside = (positions >= start) & (positions < end) & owned
        member[pl.ds(i, 1), :] = jnp.where(inside, 1.0, 0.0)
        return end

    lax.fori_loop(0, IMAGES, mark, jnp.int32(0))
    marks = member[...]
    own = jnp.sum(marks, axis=0, keepdims=True)
    marks = marks.astype(BF16)
    bias[...] = (dot(marks, marks, TN) - 1.0) * FAR
    back_by = REACH - low

    def window(array):
        return pltpu.roll(array.astype(F32), back_by, 1)[:, :WINDOW]

    for at in range(3):
        rows = slice(at * PART, (at + 1) * PART)
        joined = jnp.concatenate([qkv_l[rows, :], qkv_c[rows, :], qkv_r[rows, :]], axis=1)
        held[rows, :] = window(joined).astype(BF16)
    turned = jnp.concatenate(
        [dot(proj_ref[...], ref[...], NT).astype(BF16) for ref in (go_l, go_c, go_r)], axis=1
    )
    d_attn[...] = (window(turned) * own).astype(BF16)

    def head(q, k, v, do):
        scores = dot(k, q, TN) + bias[...]
        top = jnp.max(scores, axis=0, keepdims=True)
        weights = jnp.exp2((scores - top) * (SCALE * LOG2E))
        inverse = 1.0 / jnp.sum(weights, axis=0, keepdims=True)
        weights = weights.astype(BF16)
        attn = (dot(v, weights, NN) * (inverse * own)).astype(BF16)
        do = (do.astype(F32) * inverse).astype(BF16)
        dots = jnp.sum(do.astype(F32) * attn.astype(F32), axis=0, keepdims=True)
        dscore = (weights.astype(F32) * (dot(v, do, TN) - dots)).astype(BF16)
        return (
            attn,
            (dot(k, dscore, NN) * SCALE).astype(BF16),
            (dot(q, dscore, NT) * SCALE).astype(BF16),
            dot(do, weights, NT).astype(BF16),
        )

    def pair(at, _):
        base = pl.multiple_of(at * 2 * HEAD_DIM, 2 * HEAD_DIM)
        slabs = [held[pl.ds(a * PART + base, 2 * HEAD_DIM), :] for a in range(3)]
        slabs.append(d_attn[pl.ds(base, 2 * HEAD_DIM), :])
        both = [head(*(s[h * HEAD_DIM : (h + 1) * HEAD_DIM] for s in slabs)) for h in range(2)]
        joined = [jnp.concatenate([one, two], axis=0) for one, two in zip(*both)]
        for a in range(4):
            result[pl.ds(a * PART + base, 2 * HEAD_DIM), :] = joined[a]
        return 0

    lax.fori_loop(0, PART_HEADS // 2, pair, 0)

    for at in range(4):
        found = result[at * PART : (at + 1) * PART, :].astype(F32)
        wide = jnp.concatenate([found, jnp.zeros((PART, REACH - WINDOW), F32)], axis=1)
        wide = pltpu.roll(wide, low, 1).astype(BF16)
        if at == 0:
            attn_ref[...] = wide
        else:
            rows = slice((at - 1) * PART, at * PART)
            back_l[rows, :] = wide[:, :ROWS]
            back_c[rows, :] = wide[:, ROWS : 2 * ROWS]
            back_r[rows, :] = wide[:, 2 * ROWS :]


def attend(place, lengths, qkv, go, proj):
    block = jax.ShapeDtypeStruct((3 * PART, ROWS), BF16)
    scalar = pl.BlockSpec(memory_space=pltpu.SMEM)
    return call(
        attend_kernel,
        (jax.ShapeDtypeStruct((PART, REACH), BF16), block, block, block),
        [scalar, scalar] + [None] * 7,
        [
            pltpu.VMEM((3 * PART, WINDOW), BF16),
            pltpu.VMEM((PART, WINDOW), BF16),
            pltpu.VMEM((4 * PART, WINDOW), BF16),
            pltpu.VMEM((IMAGES, WINDOW), F32),
            pltpu.VMEM((WINDOW, WINDOW), F32),
        ],
        12 * 10**9,
    )(place, lengths, *qkv, *go, proj)


def finish_kernel(*refs):
    terms, outs = refs[: 3 * PARTS], refs[3 * PARTS :]
    for at in range(3):
        rows = slice(at * PART, (at + 1) * PART)
        whole = []
        for part in range(PARTS):
            one, two, three = (ref[rows, :].astype(F32) for ref in terms[3 * part : 3 * part + 3])
            whole.append((one + two + three).astype(BF16))
        outs[at][...] = jnp.transpose(jnp.concatenate(whole, axis=0))


def finish(terms):
    shape = jax.ShapeDtypeStruct((ROWS, WIDTH), BF16)
    return call(finish_kernel, (shape,) * 3, [None] * (3 * PARTS), [], 1 << 20)(*terms)


def send(block, axis, pairs):
    return lax.ppermute(block, axis, pairs)


def reduce_proj(part):
    seq, dp = lax.axis_index("seq"), lax.axis_index("dp")
    core, z, y, x = dp % 2, seq // 8, (seq // 4) % 2, seq % 4
    part = part.reshape(4, 2, 144, WIDTH)
    cores = [(i, i ^ 1) for i in range(4)]
    pick = lambda a, i, axis: lax.dynamic_index_in_dim(a, i, axis, keepdims=False)
    total = pick(part, core, 1) + send(pick(part, 1 - core, 1).astype(BF16), "dp", cores).astype(F32)
    for step, place, count in ((8, z, 4), (1, x, 4)):
        if step == 1:
            total = total.reshape(4, 36, WIDTH)
        summed = pick(total, place, 0)
        for k in range(1, count):
            ring = [
                (i, i - (i // step % 4) * step + ((i // step + k) % 4) * step) for i in range(32)
            ]
            summed = summed + send(pick(total, (place + k) % 4, 0).astype(BF16), "seq", ring).astype(F32)
        total = summed
    total = total + send(total, "seq", [(i, i ^ 4) for i in range(32)])
    total = total + send(total, "dp", [(i, i ^ 2) for i in range(4)])
    other = send(total, "dp", cores)
    return jnp.where(core == y, total, other)


def per_device(query, key, value, grad_out, out_proj, lengths):
    count = lax.axis_size("seq")
    ahead = [(i, i + 1) for i in range(count - 1)]
    behind = [(i + 1, i) for i in range(count - 1)]
    place = lax.axis_index("seq").reshape(1)

    def around(block):
        return send(block, "seq", ahead), block, send(block, "seq", behind)

    go = around(grad_out[0])
    halves = [around(half) for half in turn(query[0], key[0], value[0])]
    proj = jnp.transpose(out_proj)
    terms, attn = [], []
    for part in range(PARTS):
        mine = proj[part * PART : (part + 1) * PART]
        found, back_l, back_c, back_r = attend(place, lengths, halves[part], go, mine)
        attn.append(found)
        terms += [send(back_r, "seq", ahead), back_c, send(back_l, "seq", behind)]
    attn = jnp.concatenate(attn, axis=0)
    part = dot(jnp.concatenate(go, axis=0), attn, (((0,), (1,)), ((), ())))
    grad_proj = reduce_proj(part)
    grads = [g[None] for g in finish(terms)]
    return (*grads, grad_proj)


def solution(mesh):
    rows = P("dp", "seq", None)
    return jax.shard_map(
        per_device,
        mesh=mesh,
        in_specs=(rows, rows, rows, rows, P(), P("dp", None)),
        out_specs=(rows, rows, rows, P("seq", None)),
        check_vma=False,
    )
```

```python
import jax
import jax.numpy as jnp
from jax import lax
from jax.experimental import pallas as pl
from jax.experimental.pallas import tpu as pltpu
from jax.sharding import PartitionSpec as P

HEADS = 16
HEAD_DIM = 72
ROWS = 256
WIDTH = 1152
IMAGES = 32
GROUP = 8
PAIR = 2 * HEAD_DIM
SLAB = 4 * PAIR
GRADS = 3 * PAIR
SPAN = GROUP * ROWS
WINDOW = 512
REACH = WINDOW + 128
FRAME = SPAN + WINDOW
EDGE = 2 * WINDOW
SCALE = HEAD_DIM ** (-0.5)
LOG2E = 1.4426950408889634
FAR = 1e30
BF16 = jnp.bfloat16
F32 = jnp.float32
VMEM_LIMIT = 56 * 1024 * 1024

NN = (((1,), (0,)), ((), ()))
NT = (((1,), (1,)), ((), ()))
TN = (((0,), (0,)), ((), ()))
TNT = (((0,), (1,)), ((), ()))
SCALAR = pl.BlockSpec(memory_space=pltpu.SMEM)
WHOLE = pl.BlockSpec(memory_space=pltpu.VMEM)


def dot(a, b, dims):
    return lax.dot_general(a, b, dims, preferred_element_type=F32)


def call(kernel, out_shape, in_specs, scratch, flops):
    return pl.pallas_call(
        kernel,
        out_shape=out_shape,
        in_specs=in_specs,
        out_specs=jax.tree.map(lambda _: WHOLE, out_shape),
        scratch_shapes=scratch,
        compiler_params=pltpu.CompilerParams(vmem_limit_bytes=VMEM_LIMIT),
        cost_estimate=pl.CostEstimate(flops=flops, bytes_accessed=1000, transcendentals=0),
    )


def pack_kernel(q_ref, k_ref, v_ref, go_ref, proj_ref, out_ref, go_out):
    go = jnp.transpose(go_ref[...])
    for g in range(GROUP):
        for z in range(4):
            at = (2 * z + g // 4) * PAIR
            go_out[g, z * PAIR : (z + 1) * PAIR, :] = go[at : at + PAIR]
    d_attn = dot(proj_ref[...], go, TN).astype(BF16)
    turned = [jnp.transpose(ref[...]) for ref in (q_ref, k_ref, v_ref)] + [d_attn]
    for at in range(4):
        for g in range(GROUP):
            out_ref[g, at * PAIR : (at + 1) * PAIR, :] = turned[at][g * PAIR : (g + 1) * PAIR]


def pack(q, k, v, go, proj):
    shape = jax.ShapeDtypeStruct((GROUP, SLAB, ROWS), BF16)
    return call(pack_kernel, (shape, shape), [WHOLE] * 5, [], 4 * 10**9)(q, k, v, go, proj)


def attend(slab, marks):
    own = jnp.sum(marks, axis=0, keepdims=True)
    marks = marks.astype(BF16)
    bias = (dot(marks, marks, TN) - 1.0) * FAR
    heads = []
    for h in range(2):
        q, k, v, do = (
            slab[a * PAIR + h * HEAD_DIM : a * PAIR + (h + 1) * HEAD_DIM] for a in range(4)
        )
        heads.append((q, k.astype(BF16), v.astype(BF16), do * own))
    scores = [dot(k, q.astype(BF16), TN) + bias for q, k, v, do in heads]
    dprob = [dot(v, do.astype(BF16), TN) for q, k, v, do in heads]
    found = [[], [], [], []]
    for h, (q, k, v, do) in enumerate(heads):
        top = jnp.max(scores[h], axis=0, keepdims=True)
        weights = jnp.exp2((scores[h] - top) * (SCALE * LOG2E))
        inverse = 1.0 / jnp.sum(weights, axis=0, keepdims=True)
        weights = weights.astype(BF16)
        attn = (dot(v, weights, NN) * (inverse * own)).astype(BF16).astype(F32)
        dots = jnp.sum(do * attn, axis=0, keepdims=True)
        dscore = (weights.astype(F32) * (dprob[h] - dots)).astype(BF16)
        found[0].append(dot(k, dscore, NN) * (inverse * SCALE))
        found[1].append(dot((q * inverse).astype(BF16), dscore, NT) * SCALE)
        found[2].append(dot((do * inverse).astype(BF16), weights, NT))
        found[3].append(attn)
    return jnp.concatenate([one for pair in found for one in pair], axis=0)


def ends_of(length_ref):
    lengths = length_ref[...].astype(F32)
    at = lax.broadcasted_iota(jnp.int32, (IMAGES, IMAGES), 0)
    of = lax.broadcasted_iota(jnp.int32, (IMAGES, IMAGES), 1)
    ends = jnp.sum(jnp.where(of <= at, lengths, 0.0), axis=1, keepdims=True)
    starts = jnp.sum(jnp.where(of < at, lengths, 0.0), axis=1, keepdims=True)
    return starts, ends


def marks_of(starts, ends, first, last):
    positions = (first + lax.broadcasted_iota(jnp.int32, (1, WINDOW), 1)).astype(F32)
    inside = (positions >= starts) & (positions < ends)
    whole = (starts >= first.astype(F32)) & (ends <= last.astype(F32))
    return jnp.where(inside & whole, 1.0, 0.0)


def split(total, grads_ref, attn_ref):
    for b in range(GROUP):
        columns = slice(b * ROWS, (b + 1) * ROWS)
        grads_ref[b] = total[:GRADS, columns]
        attn_ref[:, columns] = total[GRADS:, columns]


def inner_kernel(place_ref, count_ref, length_ref, mid_ref, grads_ref, attn_ref, frame, total, window):
    base = place_ref[0] * SPAN

    def scan(i, carry):
        start, n, first = carry
        end = start + count_ref[0, i]
        inside = (start >= base) & (end <= base + SPAN)
        opens = inside & ((n == 0) | (end - first > WINDOW))
        n = jnp.where(opens, n + 1, n)
        first = jnp.where(opens, start, first)

        @pl.when(inside)
        def _():
            window[0, n - 1] = first
            window[1, n - 1] = end

        return end, n, first

    _, count, _ = lax.fori_loop(0, IMAGES, scan, (jnp.int32(0), jnp.int32(0), jnp.int32(0)))
    for b in range(GROUP):
        frame[:, b * ROWS : (b + 1) * ROWS] = mid_ref[b]
    frame[:, SPAN:] = jnp.zeros((SLAB, WINDOW), BF16)
    total[...] = jnp.zeros((SLAB, FRAME), BF16)
    starts, ends = ends_of(length_ref)

    def body(n, _):
        first, last = window[0, n], window[1, n]
        offset = first - base
        low = pl.multiple_of(offset // 128 * 128, 128)
        slab = frame[:, pl.ds(low, REACH)].astype(F32)
        slab = pltpu.roll(slab, lax.rem(REACH - (offset - low), REACH), 1)[:, :WINDOW]
        found = attend(slab, marks_of(starts, ends, first, last))
        wide = jnp.concatenate([found, jnp.zeros((SLAB, REACH - WINDOW), F32)], axis=1)
        wide = pltpu.roll(wide, offset - low, 1)
        old = total[:, pl.ds(low, REACH)].astype(F32)
        total[:, pl.ds(low, REACH)] = (old + wide).astype(BF16)
        return 0

    lax.fori_loop(0, count, body, 0)
    split(total[:, :SPAN], grads_ref, attn_ref)


RESULT = (
    jax.ShapeDtypeStruct((GROUP, GRADS, ROWS), BF16),
    jax.ShapeDtypeStruct((PAIR, SPAN), BF16),
)


def inner(place, lengths, mid):
    scratch = [
        pltpu.VMEM((SLAB, FRAME), BF16),
        pltpu.VMEM((SLAB, FRAME), BF16),
        pltpu.SMEM((2, IMAGES), jnp.int32),
    ]
    specs = [SCALAR, SCALAR, WHOLE, WHOLE]
    return call(inner_kernel, RESULT, specs, scratch, 20 * 10**9)(place, lengths, lengths, mid)


def edge_kernel(
    place_ref, count_ref, length_ref, mid_ref, left_ref, right_ref, grads_in, grads_ref, attn_ref, frame
):
    side = pl.program_id(0)
    border = (place_ref[0] + side) * SPAN
    grads_ref[...] = grads_in[...]
    attn_ref[...] = jnp.zeros((PAIR, WINDOW), BF16)

    def scan(i, carry):
        start, first, last = carry
        end = start + count_ref[0, i]
        over = (start < border) & (end > border)
        return end, jnp.where(over, start, first), jnp.where(over, end, last)

    nothing = jnp.int32(-1)
    _, first, last = lax.fori_loop(0, IMAGES, scan, (jnp.int32(0), nothing, nothing))

    @pl.when(last > 0)
    def _():
        def lay(blocks):
            for at, block in enumerate(blocks):
                frame[:, at * ROWS : (at + 1) * ROWS] = block

        @pl.when(side == 0)
        def _():
            lay([left_ref[0], left_ref[1], mid_ref[0], mid_ref[1]])

        @pl.when(side == 1)
        def _():
            lay([mid_ref[0], mid_ref[1], right_ref[0], right_ref[1]])

        starts, ends = ends_of(length_ref)
        offset = first - (border - WINDOW)
        slab = pltpu.roll(frame[...].astype(F32), EDGE - offset, 1)[:, :WINDOW]
        found = attend(slab, marks_of(starts, ends, first, last))
        wide = jnp.concatenate([found, jnp.zeros((SLAB, EDGE - WINDOW), F32)], axis=1)
        frame[...] = pltpu.roll(wide, offset, 1).astype(BF16)
        mine = frame[:, pl.ds(pl.multiple_of((1 - side) * WINDOW, WINDOW), WINDOW)]
        attn_ref[...] = mine[GRADS:]
        for at in range(2):
            term = mine[:GRADS, at * ROWS : (at + 1) * ROWS]
            grads_ref[at] = (grads_in[at].astype(F32) + term.astype(F32)).astype(BF16)


def edge(place, lengths, mid, left, right, grads):
    ends = lambda rows: pl.BlockSpec((2, rows, ROWS), lambda i: (i * (GROUP // 2 - 1), 0, 0))
    halo = pl.BlockSpec((2, SLAB, ROWS), lambda i: (0, 0, 0))
    return pl.pallas_call(
        edge_kernel,
        grid=(2,),
        out_shape=(RESULT[0], jax.ShapeDtypeStruct((PAIR, EDGE), BF16)),
        in_specs=[
            SCALAR, SCALAR, pl.BlockSpec((1, IMAGES), lambda i: (0, 0)),
            ends(SLAB), halo, halo, ends(GRADS),
        ],
        out_specs=(ends(GRADS), pl.BlockSpec((PAIR, WINDOW), lambda i: (0, i))),
        scratch_shapes=[pltpu.VMEM((SLAB, EDGE), BF16)],
        input_output_aliases={6: 0},
        compiler_params=pltpu.CompilerParams(
            vmem_limit_bytes=VMEM_LIMIT, dimension_semantics=("arbitrary",)
        ),
        cost_estimate=pl.CostEstimate(flops=8 * 10**9, bytes_accessed=4 << 20, transcendentals=0),
    )(place, lengths, lengths, mid, left, right, grads)


def unpack_kernel(back_ref, *out_refs):
    for at, out_ref in enumerate(out_refs):
        rows = slice(at * PAIR, (at + 1) * PAIR)
        whole = jnp.concatenate([back_ref[g, rows, :] for g in range(GROUP)], axis=0)
        out_ref[...] = jnp.transpose(whole)


def unpack(back):
    shape = jax.ShapeDtypeStruct((ROWS, WIDTH), BF16)
    return call(unpack_kernel, (shape,) * 3, [WHOLE], [], 1 << 20)(back)


def columns_of(half_ref, mine_ref, other_ref):
    first = half_ref[0] == 0
    mine, other = mine_ref[...], other_ref[...]
    return jnp.concatenate([jnp.where(first, mine, other), jnp.where(first, other, mine)], axis=0)


def inner_proj_kernel(half_ref, rows_ref, mine_ref, other_ref, out_ref):
    attn = columns_of(half_ref, mine_ref, other_ref)
    total = jnp.zeros((SLAB, 2 * PAIR), F32)
    for b in range(GROUP):
        total = total + dot(rows_ref[b], attn[:, b * ROWS : (b + 1) * ROWS], NT)
    out_ref[...] = total


def inner_proj(half, rows, mine, other):
    shape = jax.ShapeDtypeStruct((SLAB, 2 * PAIR), F32)
    specs = [SCALAR] + [WHOLE] * 3
    return call(inner_proj_kernel, shape, specs, [], 1000)(half, rows, mine, other)


def edge_proj_kernel(half_ref, low_ref, high_ref, mine_ref, other_ref, total_ref, out_ref):
    attn = columns_of(half_ref, mine_ref, other_ref)
    total = total_ref[...]
    for b in range(2):
        total = total + dot(low_ref[b], attn[:, b * ROWS : (b + 1) * ROWS], NT)
        total = total + dot(high_ref[b], attn[:, WINDOW + b * ROWS : WINDOW + (b + 1) * ROWS], NT)
    total = total.astype(BF16)
    for z in range(4):
        out_ref[z] = total[z * PAIR : (z + 1) * PAIR]


def edge_proj(half, rows, mine, other, total):
    pick = lambda at: pl.BlockSpec((2, SLAB, ROWS), lambda i: (at, 0, 0))
    whole = lambda *shape: pl.BlockSpec(shape, lambda i: (0,) * len(shape))
    return pl.pallas_call(
        edge_proj_kernel,
        grid=(1,),
        out_shape=jax.ShapeDtypeStruct((4, PAIR, 2 * PAIR), BF16),
        in_specs=[
            SCALAR, pick(0), pick(GROUP // 2 - 1),
            whole(PAIR, EDGE), whole(PAIR, EDGE), whole(SLAB, 2 * PAIR),
        ],
        out_specs=whole(4, PAIR, 2 * PAIR),
        compiler_params=pltpu.CompilerParams(
            vmem_limit_bytes=VMEM_LIMIT, dimension_semantics=("arbitrary",)
        ),
        cost_estimate=pl.CostEstimate(flops=1000, bytes_accessed=1000, transcendentals=0),
    )(half, rows, rows, mine, other, total)


def per_device(query, key, value, grad_out, out_proj, lengths):
    seq = lax.axis_index("seq")
    place = (seq // GROUP).reshape(1)
    half = ((seq // 4) % 2).reshape(1)
    count = lax.axis_size("seq")
    within_z = [[GROUP * z + g for g in range(GROUP)] for z in range(4)]

    def shift(block, by):
        return lax.ppermute(block, "seq", [(i, i + by) for i in range(count) if 0 <= i + by < count])

    def swap(block, axis, by):
        return lax.ppermute(block, axis, [(i, i ^ by) for i in range(lax.axis_size(axis))])

    def exchange(blocks, groups):
        return lax.all_to_all(blocks, "seq", 0, 0, axis_index_groups=groups)

    packed, rows = pack(query[0], key[0], value[0], grad_out[0], out_proj)
    mid = exchange(packed, within_z)
    left = shift(mid[GROUP - 2 :], GROUP)
    right = shift(mid[:2], -GROUP)
    rows, mid = lax.optimization_barrier((rows, mid))
    rows = exchange(rows, within_z)
    grads, attn = inner(place, lengths, mid)
    other = swap(attn, "seq", 4)
    grads, edges = edge(place, lengths, mid, left, right, grads)
    across = swap(edges, "seq", 4)
    grads, other, across = lax.optimization_barrier((grads, other, across))
    grads = exchange(grads, within_z)
    part = inner_proj(half, rows, attn, other)
    part = edge_proj(half, rows, edges, across, part)

    def others(blocks, step):
        at = (seq // step) % 4
        ring = lambda k: [
            (i, i + ((i // step + k) % 4 - i // step % 4) * step) for i in range(count)
        ]
        pick = lambda k: lax.dynamic_index_in_dim(blocks, (at + k) % 4, 0, keepdims=False)
        return [pick(0)] + [lax.ppermute(pick(k), "seq", ring(k)) for k in range(1, 4)]

    part = sum(one.astype(F32) for one in others(part, GROUP))
    part, grads = lax.optimization_barrier((part, grads))
    found = others(part.reshape(4, 36, 2 * PAIR), 1)
    x = seq % 4
    found = jnp.stack([found[0], *found[:0:-1]])
    found = jnp.roll(found, x, axis=0).reshape(4, 36, 2, PAIR)
    part = jnp.transpose(found, (1, 2, 0, 3)).reshape(36, WIDTH)
    part = part + swap(part, "dp", 2)
    part = part + swap(part, "dp", 1)
    return (*(g[None] for g in unpack(grads)), part)


def solution(mesh):
    rows = P("dp", "seq", None)
    return jax.shard_map(
        per_device,
        mesh=mesh,
        in_specs=(rows, rows, rows, rows, P(), P("dp", None)),
        out_specs=(rows, rows, rows, P("seq", None)),
        check_vma=False,
    )
```

```python
import jax
import jax.numpy as jnp
from jax import lax
from jax.experimental import pallas as pl
from jax.experimental.pallas import tpu as pltpu
from jax.sharding import PartitionSpec as P

HEADS = 16
HEAD_DIM = 72
ROWS = 256
WIDTH = 1152
IMAGES = 32
GROUP = 8
PAIR = 2 * HEAD_DIM
SLAB = 4 * PAIR
GRADS = 3 * PAIR
SPAN = GROUP * ROWS
WINDOW = 512
SIZES = (256, 384, WINDOW)
FILL = 256
FRAME = SPAN + WINDOW
EDGE = 2 * WINDOW
SCALE = HEAD_DIM ** (-0.5)
LOG2E = 1.4426950408889634
FAR = 1e30
BF16 = jnp.bfloat16
F32 = jnp.float32
VMEM_LIMIT = 56 * 1024 * 1024

NN = (((1,), (0,)), ((), ()))
NT = (((1,), (1,)), ((), ()))
TN = (((0,), (0,)), ((), ()))
TNT = (((0,), (1,)), ((), ()))
SCALAR = pl.BlockSpec(memory_space=pltpu.SMEM)
WHOLE = pl.BlockSpec(memory_space=pltpu.VMEM)


def dot(a, b, dims):
    return lax.dot_general(a, b, dims, preferred_element_type=F32)


def call(kernel, out_shape, in_specs, scratch, flops):
    return pl.pallas_call(
        kernel,
        out_shape=out_shape,
        in_specs=in_specs,
        out_specs=jax.tree.map(lambda _: WHOLE, out_shape),
        scratch_shapes=scratch,
        compiler_params=pltpu.CompilerParams(vmem_limit_bytes=VMEM_LIMIT),
        cost_estimate=pl.CostEstimate(flops=flops, bytes_accessed=1000, transcendentals=0),
    )


def pack_kernel(q_ref, k_ref, v_ref, go_ref, proj_ref, out_ref, go_out):
    go = jnp.transpose(go_ref[...])
    for g in range(GROUP):
        for z in range(4):
            at = (2 * z + g // 4) * PAIR
            go_out[g, z * PAIR : (z + 1) * PAIR, :] = go[at : at + PAIR]
    d_attn = jnp.transpose(dot(go_ref[...], proj_ref[...], NN).astype(BF16))
    turned = [jnp.transpose(ref[...]) for ref in (q_ref, k_ref, v_ref)] + [d_attn]
    for at in range(4):
        for g in range(GROUP):
            out_ref[g, at * PAIR : (at + 1) * PAIR, :] = turned[at][g * PAIR : (g + 1) * PAIR]


def pack(q, k, v, go, proj):
    shape = jax.ShapeDtypeStruct((GROUP, SLAB, ROWS), BF16)
    return call(pack_kernel, (shape, shape), [WHOLE] * 5, [], 4 * 10**9)(q, k, v, go, proj)


def attend(slab, marks):
    own = jnp.sum(marks, axis=0, keepdims=True)
    marks = marks.astype(BF16)
    bias = (dot(marks, marks, TN) - 1.0) * FAR
    heads = []
    for h in range(2):
        q, k, v, do = (
            slab[a * PAIR + h * HEAD_DIM : a * PAIR + (h + 1) * HEAD_DIM] for a in range(4)
        )
        heads.append((q, k.astype(BF16), v.astype(BF16), do * own))
    scores = [dot(k, q.astype(BF16), TN) + bias for q, k, v, do in heads]
    dprob = [dot(v, do.astype(BF16), TN) for q, k, v, do in heads]
    found = [[], [], [], []]
    for h, (q, k, v, do) in enumerate(heads):
        top = jnp.max(scores[h], axis=0, keepdims=True)
        weights = jnp.exp2((scores[h] - top) * (SCALE * LOG2E))
        inverse = 1.0 / jnp.sum(weights, axis=0, keepdims=True)
        weights = weights.astype(BF16)
        attn = (dot(v, weights, NN) * (inverse * own)).astype(BF16).astype(F32)
        dots = jnp.sum(do * attn, axis=0, keepdims=True)
        dscore = (weights.astype(F32) * (dprob[h] - dots)).astype(BF16)
        found[0].append(dot(k, dscore, NN) * (inverse * SCALE))
        found[1].append(dot((q * inverse).astype(BF16), dscore, NT) * SCALE)
        found[2].append(dot((do * inverse).astype(BF16), weights, NT))
        found[3].append(attn)
    return jnp.concatenate([one for pair in found for one in pair], axis=0)


def ends_of(length_ref):
    lengths = length_ref[...].astype(F32)
    at = lax.broadcasted_iota(jnp.int32, (IMAGES, IMAGES), 0)
    of = lax.broadcasted_iota(jnp.int32, (IMAGES, IMAGES), 1)
    ends = jnp.sum(jnp.where(of <= at, lengths, 0.0), axis=1, keepdims=True)
    starts = jnp.sum(jnp.where(of < at, lengths, 0.0), axis=1, keepdims=True)
    return starts, ends


def marks_of(starts, ends, first, last, size):
    positions = (first + lax.broadcasted_iota(jnp.int32, (1, size), 1)).astype(F32)
    inside = (positions >= starts) & (positions < ends)
    whole = (starts >= first.astype(F32)) & (ends <= last.astype(F32))
    return jnp.where(inside & whole, 1.0, 0.0)


def by_size(rows, step):
    for small, size in zip((0,) + SIZES, SIZES):

        @pl.when((rows > small) & (rows <= size))
        def _():
            step(size)


def inner_kernel(
    place_ref, count_ref, length_ref, mid_ref, grads_ref, attn_ref, frame, total, window, arrived, sent
):
    base = place_ref[0] * SPAN
    columns = [pl.ds(b * ROWS, ROWS) for b in range(GROUP)]
    loads = [
        pltpu.make_async_copy(mid_ref.at[b], frame.at[:, columns[b]], arrived.at[b])
        for b in range(GROUP)
    ]
    for load in loads:
        load.start()

    def scan(i, carry):
        start, n, first = carry
        end = start + count_ref[0, i]
        inside = (start >= base) & (end <= base + SPAN)
        opens = inside & ((n == 0) | (end - first > FILL))
        n = jnp.where(opens, n + 1, n)
        first = jnp.where(opens, start, first)

        @pl.when(inside)
        def _():
            window[0, n - 1] = first
            window[1, n - 1] = end

        return end, n, first

    _, count, _ = lax.fori_loop(0, IMAGES, scan, (jnp.int32(0), jnp.int32(0), jnp.int32(0)))
    frame[:, SPAN:] = jnp.zeros((SLAB, WINDOW), BF16)
    total[...] = jnp.zeros((SLAB, FRAME), BF16)
    starts, ends = ends_of(length_ref)
    for load in loads:
        load.wait()

    def body(n, _):
        first, last = window[0, n], window[1, n]
        offset = first - base
        low = pl.multiple_of(offset // 128 * 128, 128)
        shift = offset - low

        def step(size):
            reach = size + 128
            slab = frame[:, pl.ds(low, reach)].astype(F32)
            slab = pltpu.roll(slab, lax.rem(reach - shift, reach), 1)[:, :size]
            found = attend(slab, marks_of(starts, ends, first, last, size))
            wide = jnp.concatenate([found, jnp.zeros((SLAB, 128), F32)], axis=1)
            wide = pltpu.roll(wide, shift, 1)
            old = total[:, pl.ds(low, reach)].astype(F32)
            total[:, pl.ds(low, reach)] = (old + wide).astype(BF16)

        by_size(last - first, step)
        return 0

    lax.fori_loop(0, count, body, 0)
    stores = [
        pltpu.make_async_copy(total.at[pl.ds(0, GRADS), columns[b]], grads_ref.at[b], sent.at[b])
        for b in range(GROUP)
    ]
    found = total.at[pl.ds(GRADS, PAIR), pl.ds(0, SPAN)]
    stores.append(pltpu.make_async_copy(found, attn_ref, sent.at[GROUP]))
    for store in stores:
        store.start()
    for store in stores:
        store.wait()


RESULT = (
    jax.ShapeDtypeStruct((GROUP, GRADS, ROWS), BF16),
    jax.ShapeDtypeStruct((PAIR, SPAN), BF16),
)


def inner(place, lengths, mid):
    hbm = pl.BlockSpec(memory_space=pl.ANY)
    return pl.pallas_call(
        inner_kernel,
        out_shape=RESULT,
        in_specs=[SCALAR, SCALAR, WHOLE, hbm],
        out_specs=(hbm, hbm),
        scratch_shapes=[
            pltpu.VMEM((SLAB, FRAME), BF16),
            pltpu.VMEM((SLAB, FRAME), BF16),
            pltpu.SMEM((2, IMAGES), jnp.int32),
            pltpu.SemaphoreType.DMA((GROUP,)),
            pltpu.SemaphoreType.DMA((GROUP + 1,)),
        ],
        compiler_params=pltpu.CompilerParams(vmem_limit_bytes=VMEM_LIMIT),
        cost_estimate=pl.CostEstimate(flops=20 * 10**9, bytes_accessed=4 << 20, transcendentals=0),
    )(place, lengths, lengths, mid)


def edge_kernel(
    place_ref, count_ref, length_ref, mid_ref, left_ref, right_ref, grads_in, grads_ref, attn_ref, frame
):
    side = pl.program_id(0)
    border = (place_ref[0] + side) * SPAN
    grads_ref[...] = grads_in[...]
    attn_ref[...] = jnp.zeros((PAIR, WINDOW), BF16)

    def scan(i, carry):
        start, first, last = carry
        end = start + count_ref[0, i]
        over = (start < border) & (end > border)
        return end, jnp.where(over, start, first), jnp.where(over, end, last)

    nothing = jnp.int32(-1)
    _, first, last = lax.fori_loop(0, IMAGES, scan, (jnp.int32(0), nothing, nothing))

    @pl.when(last > 0)
    def _():
        def lay(blocks):
            for at, block in enumerate(blocks):
                frame[:, at * ROWS : (at + 1) * ROWS] = block

        @pl.when(side == 0)
        def _():
            lay([left_ref[0], left_ref[1], mid_ref[0], mid_ref[1]])

        @pl.when(side == 1)
        def _():
            lay([mid_ref[0], mid_ref[1], right_ref[0], right_ref[1]])

        starts, ends = ends_of(length_ref)
        offset = first - (border - WINDOW)

        def step(size):
            slab = pltpu.roll(frame[...].astype(F32), EDGE - offset, 1)[:, :size]
            found = attend(slab, marks_of(starts, ends, first, last, size))
            wide = jnp.concatenate([found, jnp.zeros((SLAB, EDGE - size), F32)], axis=1)
            frame[...] = pltpu.roll(wide, offset, 1).astype(BF16)

        by_size(last - first, step)
        mine = frame[:, pl.ds(pl.multiple_of((1 - side) * WINDOW, WINDOW), WINDOW)]
        attn_ref[...] = mine[GRADS:]
        for at in range(2):
            term = mine[:GRADS, at * ROWS : (at + 1) * ROWS]
            grads_ref[at] = (grads_in[at].astype(F32) + term.astype(F32)).astype(BF16)


def edge(place, lengths, mid, left, right, grads):
    ends = lambda rows: pl.BlockSpec((2, rows, ROWS), lambda i: (i * (GROUP // 2 - 1), 0, 0))
    halo = pl.BlockSpec((2, SLAB, ROWS), lambda i: (0, 0, 0))
    return pl.pallas_call(
        edge_kernel,
        grid=(2,),
        out_shape=(RESULT[0], jax.ShapeDtypeStruct((PAIR, EDGE), BF16)),
        in_specs=[
            SCALAR, SCALAR, pl.BlockSpec((1, IMAGES), lambda i: (0, 0)),
            ends(SLAB), halo, halo, ends(GRADS),
        ],
        out_specs=(ends(GRADS), pl.BlockSpec((PAIR, WINDOW), lambda i: (0, i))),
        scratch_shapes=[pltpu.VMEM((SLAB, EDGE), BF16)],
        input_output_aliases={6: 0},
        compiler_params=pltpu.CompilerParams(
            vmem_limit_bytes=VMEM_LIMIT, dimension_semantics=("arbitrary",)
        ),
        cost_estimate=pl.CostEstimate(flops=8 * 10**9, bytes_accessed=4 << 20, transcendentals=0),
    )(place, lengths, lengths, mid, left, right, grads)


def unpack_kernel(back_ref, *out_refs):
    for at, out_ref in enumerate(out_refs):
        rows = slice(at * PAIR, (at + 1) * PAIR)
        whole = jnp.concatenate([back_ref[g, rows, :] for g in range(GROUP)], axis=0)
        out_ref[...] = jnp.transpose(whole)


def unpack(back):
    shape = jax.ShapeDtypeStruct((ROWS, WIDTH), BF16)
    return call(unpack_kernel, (shape,) * 3, [WHOLE], [], 1 << 20)(back)


def proj_kernel(at_ref, rows_ref, mine_ref, other_ref, edge_ref, across_ref, *refs):
    outs, total = refs[:-1], refs[-1]
    first = at_ref[1] == 0

    def columns(mine, other):
        return jnp.concatenate([jnp.where(first, mine, other), jnp.where(first, other, mine)], axis=0)

    attn = columns(mine_ref[...], other_ref[...])
    edges = columns(edge_ref[...], across_ref[...])
    low = (attn[:, :WINDOW].astype(F32) + edges[:, :WINDOW].astype(F32)).astype(BF16)
    high = (attn[:, SPAN - WINDOW :].astype(F32) + edges[:, WINDOW:].astype(F32)).astype(BF16)
    attn = jnp.concatenate([low, attn[:, WINDOW : SPAN - WINDOW], high], axis=1)
    rows = jnp.concatenate([rows_ref[b] for b in range(GROUP)], axis=1)
    total[...] = dot(rows, attn, NT)
    for k, out_ref in enumerate(outs):
        begin = pl.multiple_of(lax.rem(at_ref[0] + k, 4) * PAIR, PAIR)
        out_ref[...] = total[pl.ds(begin, PAIR), :].astype(out_ref.dtype)


def partial_proj(at, rows, mine, other, edges, across):
    block = lambda dtype: jax.ShapeDtypeStruct((PAIR, 2 * PAIR), dtype)
    shapes = (block(F32),) + (block(BF16),) * 3
    scratch = [pltpu.VMEM((SLAB, 2 * PAIR), F32)]
    specs = [SCALAR] + [WHOLE] * 5
    return call(proj_kernel, shapes, specs, scratch, 1000)(at, rows, mine, other, edges, across)


def select(blocks, at):
    return sum(jnp.where(at == j, block, 0.0) for j, block in enumerate(blocks))


def sum_z_kernel(at_ref, *refs):
    total = refs[0][...] + sum(ref[...].astype(F32) for ref in refs[1:4])
    blocks = [total[j * 36 : (j + 1) * 36] for j in range(4)]
    for k, out_ref in enumerate(refs[4:]):
        out_ref[...] = select(blocks, lax.rem(at_ref[2] + k, 4))


def sum_z(at, terms):
    shape = jax.ShapeDtypeStruct((36, 2 * PAIR), F32)
    return call(sum_z_kernel, (shape,) * 4, [SCALAR] + [WHOLE] * 4, [], 1000)(at, *terms)


def join_x_kernel(at_ref, *refs):
    terms = [ref[...] for ref in refs[:4]]
    for j in range(4):
        block = select(terms, lax.rem(at_ref[2] + 4 - j, 4))
        for y in range(2):
            begin = (4 * y + j) * PAIR
            refs[4][:, begin : begin + PAIR] = block[:, y * PAIR : (y + 1) * PAIR]


def join_x(at, terms):
    shape = jax.ShapeDtypeStruct((36, WIDTH), F32)
    return call(join_x_kernel, shape, [SCALAR] + [WHOLE] * 4, [], 1000)(at, *terms)


def per_device(query, key, value, grad_out, out_proj, lengths):
    seq = lax.axis_index("seq")
    place = jnp.stack([seq // GROUP, (seq // 4) % 2, seq % 4])
    count = lax.axis_size("seq")
    within_z = [[GROUP * z + g for g in range(GROUP)] for z in range(4)]

    def shift(block, by):
        return lax.ppermute(block, "seq", [(i, i + by) for i in range(count) if 0 <= i + by < count])

    def swap(block, axis, by):
        return lax.ppermute(block, axis, [(i, i ^ by) for i in range(lax.axis_size(axis))])

    def exchange(blocks, groups):
        return lax.all_to_all(blocks, "seq", 0, 0, axis_index_groups=groups)

    packed, rows = pack(query[0], key[0], value[0], grad_out[0], out_proj)
    mid = exchange(packed, within_z)
    left = shift(mid[GROUP - 2 :], GROUP)
    right = shift(mid[:2], -GROUP)
    rows, mid = lax.optimization_barrier((rows, mid))
    rows = exchange(rows, within_z)
    grads, attn = inner(place, lengths, mid)
    other = swap(attn, "seq", 4)
    grads, edges = edge(place, lengths, mid, left, right, grads)
    across = swap(edges, "seq", 4)
    grads, other, across = lax.optimization_barrier((grads, other, across))
    grads = exchange(grads, within_z)
    part, *away = partial_proj(place, rows, attn, other, edges, across)

    def ahead(block, step, k):
        to = lambda i: i + ((i // step + k) % 4 - i // step % 4) * step
        return lax.ppermute(block, "seq", [(i, to(i)) for i in range(count)])

    part, *away = sum_z(place, [part] + [ahead(b, GROUP, k + 1) for k, b in enumerate(away)])
    away = [ahead(b, 1, k + 1) for k, b in enumerate(away)]
    grads = unpack(grads)
    grads, away = lax.optimization_barrier((grads, away))
    part = join_x(place, [part] + away)
    part = (part + swap(part, "dp", 1)) + (swap(part, "dp", 2) + swap(part, "dp", 3))
    return (*(g[None] for g in grads), part)


def solution(mesh):
    rows = P("dp", "seq", None)
    return jax.shard_map(
        per_device,
        mesh=mesh,
        in_specs=(rows, rows, rows, rows, P(), P("dp", None)),
        out_specs=(rows, rows, rows, P("seq", None)),
        check_vma=False,
    )
```

```python
import jax
import jax.numpy as jnp
from jax import lax
from jax.experimental import pallas as pl
from jax.experimental.pallas import tpu as pltpu
from jax.sharding import PartitionSpec as P

HEADS = 16
HEAD_DIM = 72
ROWS = 256
WIDTH = 1152
IMAGES = 32
GROUP = 8
PAIR = 2 * HEAD_DIM
SLAB = 4 * PAIR
GRADS = 3 * PAIR
SPAN = GROUP * ROWS
WINDOW = 512
SIZES = (256, 384, WINDOW)
FILL = 256
FRAME = SPAN + WINDOW
EDGE = 2 * WINDOW
SCALE = HEAD_DIM ** (-0.5)
LOG2E = 1.4426950408889634
FAR = 1e30
BF16 = jnp.bfloat16
F32 = jnp.float32
VMEM_LIMIT = 24 * 1024 * 1024
ALL_VMEM = 56 * 1024 * 1024

NN = (((1,), (0,)), ((), ()))
NT = (((1,), (1,)), ((), ()))
TN = (((0,), (0,)), ((), ()))
TNT = (((0,), (1,)), ((), ()))
SCALAR = pl.BlockSpec(memory_space=pltpu.SMEM)
WHOLE = pl.BlockSpec(memory_space=pltpu.VMEM)


def dot(a, b, dims):
    return lax.dot_general(a, b, dims, preferred_element_type=F32)


def call(kernel, out_shape, in_specs, scratch, flops, limit=VMEM_LIMIT):
    return pl.pallas_call(
        kernel,
        out_shape=out_shape,
        in_specs=in_specs,
        out_specs=jax.tree.map(lambda _: WHOLE, out_shape),
        scratch_shapes=scratch,
        compiler_params=pltpu.CompilerParams(vmem_limit_bytes=limit),
        cost_estimate=pl.CostEstimate(flops=flops, bytes_accessed=1000, transcendentals=0),
    )


def pack_kernel(at_ref, q_ref, k_ref, v_ref, go_ref, proj_ref, out_ref, same_ref, other_ref, turned_go):
    turned_go[...] = jnp.transpose(go_ref[...])
    for z in range(4):
        for y, half_ref in ((at_ref[1], same_ref), (1 - at_ref[1], other_ref)):
            begin = pl.multiple_of((2 * z + y) * PAIR, PAIR)
            half_ref[z * PAIR : (z + 1) * PAIR, :] = turned_go[pl.ds(begin, PAIR), :]
    d_attn = jnp.transpose(dot(go_ref[...], proj_ref[...], NN).astype(BF16))
    turned = [jnp.transpose(ref[...]) for ref in (q_ref, k_ref, v_ref)] + [d_attn]
    for at in range(4):
        for g in range(GROUP):
            out_ref[g, at * PAIR : (at + 1) * PAIR, :] = turned[at][g * PAIR : (g + 1) * PAIR]


def pack(at, q, k, v, go, proj):
    half = jax.ShapeDtypeStruct((SLAB, ROWS), BF16)
    shapes = (jax.ShapeDtypeStruct((GROUP, SLAB, ROWS), BF16), half, half)
    scratch = [pltpu.VMEM((WIDTH, ROWS), BF16)]
    return call(pack_kernel, shapes, [SCALAR] + [WHOLE] * 5, scratch, 1000, ALL_VMEM)(
        at, q, k, v, go, proj
    )


def weigh(slab, marks):
    own = jnp.sum(marks, axis=0, keepdims=True)
    marks = marks.astype(BF16)
    bias = (dot(marks, marks, TN) - 1.0) * FAR
    heads, found = [], []
    for h in range(2):
        q, k, v, do = (
            slab[a * PAIR + h * HEAD_DIM : a * PAIR + (h + 1) * HEAD_DIM] for a in range(4)
        )
        heads.append((q, k.astype(BF16), v.astype(BF16), do * own))
    scores = [dot(k, q.astype(BF16), TN) + bias for q, k, v, do in heads]
    for (q, k, v, do), score in zip(heads, scores):
        top = jnp.max(score, axis=0, keepdims=True)
        weights = jnp.exp2((score - top) * (SCALE * LOG2E))
        inverse = 1.0 / jnp.sum(weights, axis=0, keepdims=True)
        weights = weights.astype(BF16)
        attn = (dot(v, weights, NN) * (inverse * own)).astype(BF16).astype(F32)
        found.append((weights, inverse, attn))
    return heads, found


def attend(slab, marks):
    heads, found = weigh(slab, marks)
    dprob = [dot(v, do.astype(BF16), TN) for q, k, v, do in heads]
    outs = [[], [], [], []]
    for (q, k, v, do), (weights, inverse, attn), dp in zip(heads, found, dprob):
        dots = jnp.sum(do * attn, axis=0, keepdims=True)
        dscore = (weights.astype(F32) * (dp - dots)).astype(BF16)
        outs[0].append(dot(k, dscore, NN) * (inverse * SCALE))
        outs[1].append(dot((q * inverse).astype(BF16), dscore, NT) * SCALE)
        outs[2].append(dot((do * inverse).astype(BF16), weights, NT))
        outs[3].append(attn)
    return jnp.concatenate([one for pair in outs for one in pair], axis=0)


def ends_of(length_ref):
    lengths = length_ref[...].astype(F32)
    at = lax.broadcasted_iota(jnp.int32, (IMAGES, IMAGES), 0)
    of = lax.broadcasted_iota(jnp.int32, (IMAGES, IMAGES), 1)
    ends = jnp.sum(jnp.where(of <= at, lengths, 0.0), axis=1, keepdims=True)
    starts = jnp.sum(jnp.where(of < at, lengths, 0.0), axis=1, keepdims=True)
    return starts, ends


def marks_of(starts, ends, first, last, size):
    positions = (first + lax.broadcasted_iota(jnp.int32, (1, size), 1)).astype(F32)
    inside = (positions >= starts) & (positions < ends)
    whole = (starts >= first.astype(F32)) & (ends <= last.astype(F32))
    return jnp.where(inside & whole, 1.0, 0.0)


def by_size(rows, step):
    for small, size in zip((0,) + SIZES, SIZES):

        @pl.when((rows > small) & (rows <= size))
        def _():
            step(size)


def inner_kernel(
    place_ref, count_ref, length_ref, mid_ref, grads_ref, attn_ref, frame, total, window, arrived, sent
):
    base = place_ref[0] * SPAN
    columns = [pl.ds(b * ROWS, ROWS) for b in range(GROUP)]
    loads = [
        pltpu.make_async_copy(mid_ref.at[b], frame.at[:, columns[b]], arrived.at[b])
        for b in range(GROUP)
    ]
    for load in loads:
        load.start()

    def scan(i, carry):
        start, n, first = carry
        end = start + count_ref[0, i]
        inside = (start >= base) & (end <= base + SPAN)
        opens = inside & ((n == 0) | (end - first > FILL))
        n = jnp.where(opens, n + 1, n)
        first = jnp.where(opens, start, first)

        @pl.when(inside)
        def _():
            window[0, n - 1] = first
            window[1, n - 1] = end

        return end, n, first

    _, count, _ = lax.fori_loop(0, IMAGES, scan, (jnp.int32(0), jnp.int32(0), jnp.int32(0)))
    frame[:, SPAN:] = jnp.zeros((SLAB, WINDOW), BF16)
    total[...] = jnp.zeros((SLAB, FRAME), BF16)
    starts, ends = ends_of(length_ref)
    for load in loads:
        load.wait()

    def body(n, _):
        first, last = window[0, n], window[1, n]
        offset = first - base
        low = pl.multiple_of(offset // 128 * 128, 128)
        shift = offset - low

        def step(size):
            reach = size + 128
            slab = frame[:, pl.ds(low, reach)].astype(F32)
            slab = pltpu.roll(slab, lax.rem(reach - shift, reach), 1)[:, :size]
            found = attend(slab, marks_of(starts, ends, first, last, size))
            wide = jnp.concatenate([found, jnp.zeros((SLAB, 128), F32)], axis=1)
            wide = pltpu.roll(wide, shift, 1)
            old = total[:, pl.ds(low, reach)].astype(F32)
            total[:, pl.ds(low, reach)] = (old + wide).astype(BF16)

        by_size(last - first, step)
        return 0

    lax.fori_loop(0, count, body, 0)
    stores = [
        pltpu.make_async_copy(total.at[pl.ds(0, GRADS), columns[b]], grads_ref.at[b], sent.at[b])
        for b in range(GROUP)
    ]
    found = total.at[pl.ds(GRADS, PAIR), pl.ds(0, SPAN)]
    stores.append(pltpu.make_async_copy(found, attn_ref, sent.at[GROUP]))
    for store in stores:
        store.start()
    for store in stores:
        store.wait()


RESULT = (
    jax.ShapeDtypeStruct((GROUP, GRADS, ROWS), BF16),
    jax.ShapeDtypeStruct((PAIR, SPAN), BF16),
)


def inner(place, lengths, mid):
    hbm = pl.BlockSpec(memory_space=pl.ANY)
    return pl.pallas_call(
        inner_kernel,
        out_shape=RESULT,
        in_specs=[SCALAR, SCALAR, WHOLE, hbm],
        out_specs=(pl.BlockSpec(memory_space=pltpu.HBM), hbm),
        scratch_shapes=[
            pltpu.VMEM((SLAB, FRAME), BF16),
            pltpu.VMEM((SLAB, FRAME), BF16),
            pltpu.SMEM((2, IMAGES), jnp.int32),
            pltpu.SemaphoreType.DMA((GROUP,)),
            pltpu.SemaphoreType.DMA((GROUP + 1,)),
        ],
        compiler_params=pltpu.CompilerParams(vmem_limit_bytes=VMEM_LIMIT),
        cost_estimate=pl.CostEstimate(flops=1000, bytes_accessed=1000, transcendentals=0),
    )(place, lengths, lengths, mid)


def edge_image(place_ref, count_ref, length_ref, mid_ref, left_ref, right_ref, frame, step):
    side = pl.program_id(0)
    border = (place_ref[0] + side) * SPAN

    def scan(i, carry):
        start, first, last = carry
        end = start + count_ref[0, i]
        over = (start < border) & (end > border)
        return end, jnp.where(over, start, first), jnp.where(over, end, last)

    nothing = jnp.int32(-1)
    _, first, last = lax.fori_loop(0, IMAGES, scan, (jnp.int32(0), nothing, nothing))

    @pl.when(last > 0)
    def _():
        def lay(blocks):
            for at, block in enumerate(blocks):
                frame[:, at * ROWS : (at + 1) * ROWS] = block

        @pl.when(side == 0)
        def _():
            lay([left_ref[0], left_ref[1], mid_ref[0], mid_ref[1]])

        @pl.when(side == 1)
        def _():
            lay([mid_ref[0], mid_ref[1], right_ref[0], right_ref[1]])

        starts, ends = ends_of(length_ref)
        offset = first - (border - WINDOW)

        def sized(size):
            slab = pltpu.roll(frame[...].astype(F32), EDGE - offset, 1)[:, :size]
            found = step(slab, marks_of(starts, ends, first, last, size))
            count = found.shape[0]
            wide = jnp.concatenate([found, jnp.zeros((count, EDGE - size), F32)], axis=1)
            frame[:count, :] = pltpu.roll(wide, offset, 1).astype(BF16)

        by_size(last - first, sized)

    @pl.when(last <= 0)
    def _():
        frame[...] = jnp.zeros((SLAB, EDGE), BF16)

    return pl.ds(pl.multiple_of((1 - side) * WINDOW, WINDOW), WINDOW)


def edge_attn_kernel(place_ref, count_ref, length_ref, mid_ref, left_ref, right_ref, attn_ref, frame):
    def step(slab, marks):
        return jnp.concatenate([attn for _, _, attn in weigh(slab, marks)[1]], axis=0)

    mine = edge_image(place_ref, count_ref, length_ref, mid_ref, left_ref, right_ref, frame, step)
    attn_ref[...] = frame[:PAIR, mine]


def edge_grads_kernel(
    place_ref, count_ref, length_ref, mid_ref, left_ref, right_ref, grads_in, *more
):
    grads_ref, frame = more[-2:]
    mine = edge_image(place_ref, count_ref, length_ref, mid_ref, left_ref, right_ref, frame, attend)
    found = frame[:GRADS, mine]
    for at in range(2):
        term = found[:, at * ROWS : (at + 1) * ROWS]
        grads_ref[at] = (grads_in[at].astype(F32) + term.astype(F32)).astype(BF16)


def edge(place, lengths, mid, left, right, grads=None, after=()):
    ends = lambda rows: pl.BlockSpec((2, rows, ROWS), lambda i: (i * (GROUP // 2 - 1), 0, 0))
    halo = pl.BlockSpec((2, SLAB, ROWS), lambda i: (0, 0, 0))
    specs = [SCALAR, SCALAR, pl.BlockSpec((1, IMAGES), lambda i: (0, 0)), ends(SLAB), halo, halo]
    args = (place, lengths, lengths, mid, left, right)
    more = dict(
        grid=(2,),
        scratch_shapes=[pltpu.VMEM((SLAB, EDGE), BF16)],
        compiler_params=pltpu.CompilerParams(
            vmem_limit_bytes=VMEM_LIMIT, dimension_semantics=("arbitrary",)
        ),
        cost_estimate=pl.CostEstimate(flops=1000, bytes_accessed=1000, transcendentals=0),
    )
    if grads is None:
        return pl.pallas_call(
            edge_attn_kernel,
            out_shape=jax.ShapeDtypeStruct((PAIR, EDGE), BF16),
            in_specs=specs,
            out_specs=pl.BlockSpec((PAIR, WINDOW), lambda i: (0, i)),
            **more,
        )(*args)
    return pl.pallas_call(
        edge_grads_kernel,
        out_shape=RESULT[0],
        in_specs=specs + [ends(GRADS)] + [pl.BlockSpec(memory_space=pl.ANY)] * len(after),
        out_specs=ends(GRADS),
        input_output_aliases={6: 0},
        **more,
    )(*args, grads, *after)


def unpack_kernel(back_ref, *out_refs):
    for at, out_ref in enumerate(out_refs):
        rows = slice(at * PAIR, (at + 1) * PAIR)
        whole = jnp.concatenate([back_ref[g, rows, :] for g in range(GROUP)], axis=0)
        out_ref[...] = jnp.transpose(whole)


def unpack(back):
    shape = jax.ShapeDtypeStruct((ROWS, WIDTH), BF16)
    return call(unpack_kernel, (shape,) * 3, [WHOLE], [], 1000)(back)


def proj_kernel(at_ref, mine_ref, other_ref, edge_ref, across_ref, _, *refs):
    rows, outs, (attn, total) = refs[:4], refs[4:-2], refs[-2:]
    first = at_ref[1] == 0

    def columns(mine, other):
        return jnp.concatenate([jnp.where(first, mine, other), jnp.where(first, other, mine)], axis=0)

    inner_attn = columns(mine_ref[...], other_ref[...])
    edges = columns(edge_ref[...], across_ref[...]).astype(F32)
    low = inner_attn[:, :WINDOW].astype(F32) + edges[:, :WINDOW]
    high = inner_attn[:, SPAN - WINDOW :].astype(F32) + edges[:, WINDOW:]
    attn[:, :WINDOW] = low.astype(BF16)
    attn[:, WINDOW : SPAN - WINDOW] = inner_attn[:, WINDOW : SPAN - WINDOW]
    attn[:, SPAN - WINDOW :] = high.astype(BF16)
    found = jnp.zeros((SLAB, 2 * PAIR), F32)
    for k in range(GROUP):
        begin = pl.multiple_of((at_ref[3] ^ k) * ROWS, ROWS)
        part = rows[k % 4][k // 4 * SLAB : (k // 4 + 1) * SLAB, :]
        found = found + dot(part, attn[:, pl.ds(begin, ROWS)], NT)
    total[...] = found
    for k, out_ref in enumerate(outs):
        begin = pl.multiple_of(lax.rem(at_ref[0] + k, 4) * PAIR, PAIR)
        out_ref[...] = total[pl.ds(begin, PAIR), :].astype(out_ref.dtype)


def partial_proj(at, rows, mine, other, edges, across, token):
    block = lambda dtype: jax.ShapeDtypeStruct((PAIR, 2 * PAIR), dtype)
    shapes = (block(F32),) + (block(BF16),) * 3
    scratch = [pltpu.VMEM((2 * PAIR, SPAN), BF16), pltpu.VMEM((SLAB, 2 * PAIR), F32)]
    specs = [SCALAR] + [WHOLE] * 4 + [pl.BlockSpec(memory_space=pl.ANY)] + [WHOLE] * 4
    args = (at, mine, other, edges, across, token, *rows)
    return call(proj_kernel, shapes, specs, scratch, 1000, ALL_VMEM)(*args)


def select(blocks, at):
    return sum(jnp.where(at == j, block, 0.0) for j, block in enumerate(blocks))


def sum_z_kernel(at_ref, *refs):
    total = refs[0][...] + sum(ref[...].astype(F32) for ref in refs[1:4])
    blocks = [total[j * 36 : (j + 1) * 36] for j in range(4)]
    for k, out_ref in enumerate(refs[4:]):
        out_ref[...] = select(blocks, lax.rem(at_ref[2] + k, 4))


def sum_z(at, terms):
    shape = jax.ShapeDtypeStruct((36, 2 * PAIR), F32)
    return call(sum_z_kernel, (shape,) * 4, [SCALAR] + [WHOLE] * 4, [], 1000)(at, *terms)


def join_x_kernel(at_ref, *refs):
    terms = [ref[...] for ref in refs[:4]]
    for j in range(4):
        block = select(terms, lax.rem(at_ref[2] + 4 - j, 4))
        for y in range(2):
            begin = (4 * y + j) * PAIR
            refs[4][:, begin : begin + PAIR] = block[:, y * PAIR : (y + 1) * PAIR]


def join_x(at, terms):
    shape = jax.ShapeDtypeStruct((36, WIDTH), F32)
    return call(join_x_kernel, shape, [SCALAR] + [WHOLE] * 4, [], 1000)(at, *terms)


def per_device(query, key, value, grad_out, out_proj, lengths):
    seq = lax.axis_index("seq")
    place = jnp.stack([seq // GROUP, (seq // 4) % 2, seq % 4, seq % GROUP])
    count = lax.axis_size("seq")
    within_z = [[GROUP * z + g for g in range(GROUP)] for z in range(4)]

    def shift(block, by):
        return lax.ppermute(block, "seq", [(i, i + by) for i in range(count) if 0 <= i + by < count])

    def corner(block):
        return block[:16, :128]

    def swap(block, axis, by):
        return lax.ppermute(block, axis, [(i, i ^ by) for i in range(lax.axis_size(axis))])

    def exchange(blocks, groups):
        return lax.all_to_all(blocks, "seq", 0, 0, axis_index_groups=groups)

    packed, same, across_y = pack(place, query[0], key[0], value[0], grad_out[0], out_proj)
    mid = exchange(packed, within_z)
    rows = jnp.concatenate([same, swap(across_y, "seq", 4)], axis=0)
    rows = [rows] + [swap(rows, "seq", k) for k in range(1, 4)]
    tokens = [corner(block) for block in rows[1:]]
    left = shift(mid[GROUP - 2 :], GROUP)
    right = shift(mid[:2], -GROUP)
    grads, attn = inner(place, lengths, mid)
    other = swap(attn, "seq", 4)
    edges = edge(place, lengths, mid, left, right)
    across = swap(edges, "seq", 4)
    grads = edge(place, lengths, mid, left, right, grads, [edges] + tokens)
    token = corner(other) + corner(across)
    grads, token = lax.optimization_barrier((grads, token))
    grads = exchange(grads, within_z)
    part, *away = partial_proj(place, rows, attn, other, edges, across, token)

    def ahead(block, step, k):
        to = lambda i: i + ((i // step + k) % 4 - i // step % 4) * step
        return lax.ppermute(block, "seq", [(i, to(i)) for i in range(count)])

    part, *away = sum_z(place, [part] + [ahead(b, GROUP, k + 1) for k, b in enumerate(away)])
    away = [ahead(b, 1, k + 1) for k, b in enumerate(away)]
    grads = unpack(grads)
    grads, away = lax.optimization_barrier((grads, away))
    part = join_x(place, [part] + away)
    part = (part + swap(part, "dp", 1)) + (swap(part, "dp", 2) + swap(part, "dp", 3))
    return (*(g[None] for g in grads), part)


def solution(mesh):
    rows = P("dp", "seq", None)
    return jax.shard_map(
        per_device,
        mesh=mesh,
        in_specs=(rows, rows, rows, rows, P(), P("dp", None)),
        out_specs=(rows, rows, rows, P("seq", None)),
        check_vma=False,
    )
```

```python
import jax
import jax.numpy as jnp
from jax import lax
from jax.experimental import pallas as pl
from jax.experimental.pallas import tpu as pltpu
from jax.sharding import PartitionSpec as P

HEADS = 16
HEAD_DIM = 72
ROWS = 256
WIDTH = 1152
IMAGES = 32
GROUP = 8
PAIR = 2 * HEAD_DIM
SLAB = 4 * PAIR
GRADS = 3 * PAIR
SPAN = GROUP * ROWS
WINDOW = 512
SIZES = (256, 384, WINDOW)
FILL = 256
FRAME = SPAN + WINDOW
EDGE = 2 * WINDOW
SCALE = HEAD_DIM ** (-0.5)
LOG2E = 1.4426950408889634
FAR = 1e30
BF16 = jnp.bfloat16
F32 = jnp.float32
VMEM_LIMIT = 24 * 1024 * 1024
ALL_VMEM = 56 * 1024 * 1024

NN = (((1,), (0,)), ((), ()))
NT = (((1,), (1,)), ((), ()))
TN = (((0,), (0,)), ((), ()))
TNT = (((0,), (1,)), ((), ()))
SCALAR = pl.BlockSpec(memory_space=pltpu.SMEM)
WHOLE = pl.BlockSpec(memory_space=pltpu.VMEM)


def dot(a, b, dims):
    return lax.dot_general(a, b, dims, preferred_element_type=F32)


def call(kernel, out_shape, in_specs, scratch, flops, limit=VMEM_LIMIT):
    return pl.pallas_call(
        kernel,
        out_shape=out_shape,
        in_specs=in_specs,
        out_specs=jax.tree.map(lambda _: WHOLE, out_shape),
        scratch_shapes=scratch,
        compiler_params=pltpu.CompilerParams(vmem_limit_bytes=limit),
        cost_estimate=pl.CostEstimate(flops=flops, bytes_accessed=1000, transcendentals=0),
    )


def pack_kernel(q_ref, k_ref, v_ref, go_ref, proj_ref, out_ref, *halves):
    go = jnp.transpose(go_ref[...])
    for y, half_ref in enumerate(halves):
        for z in range(4):
            half_ref[z * PAIR : (z + 1) * PAIR, :] = go[(2 * z + y) * PAIR : (2 * z + y + 1) * PAIR]
    d_attn = jnp.transpose(dot(go_ref[...], proj_ref[...], NN).astype(BF16))
    turned = [jnp.transpose(ref[...]) for ref in (q_ref, k_ref, v_ref)] + [d_attn]
    for at in range(4):
        for g in range(GROUP):
            out_ref[g, at * PAIR : (at + 1) * PAIR, :] = turned[at][g * PAIR : (g + 1) * PAIR]


def pack(q, k, v, go, proj):
    half = jax.ShapeDtypeStruct((SLAB, ROWS), BF16)
    shapes = (jax.ShapeDtypeStruct((GROUP, SLAB, ROWS), BF16), half, half)
    return call(pack_kernel, shapes, [WHOLE] * 5, [], 1000, ALL_VMEM)(q, k, v, go, proj)


def weigh(slab, marks):
    own = jnp.sum(marks, axis=0, keepdims=True)
    marks = marks.astype(BF16)
    bias = (dot(marks, marks, TN) - 1.0) * FAR
    heads, found = [], []
    for h in range(2):
        q, k, v, do = (
            slab[a * PAIR + h * HEAD_DIM : a * PAIR + (h + 1) * HEAD_DIM] for a in range(4)
        )
        heads.append((q, k.astype(BF16), v.astype(BF16), do * own))
    scores = [dot(k, q.astype(BF16), TN) + bias for q, k, v, do in heads]
    for (q, k, v, do), score in zip(heads, scores):
        top = jnp.max(score, axis=0, keepdims=True)
        weights = jnp.exp2((score - top) * (SCALE * LOG2E))
        inverse = 1.0 / jnp.sum(weights, axis=0, keepdims=True)
        weights = weights.astype(BF16)
        attn = (dot(v, weights, NN) * (inverse * own)).astype(BF16).astype(F32)
        found.append((weights, inverse, attn))
    return heads, found


def attend(slab, marks):
    heads, found = weigh(slab, marks)
    dprob = [dot(v, do.astype(BF16), TN) for q, k, v, do in heads]
    outs = [[], [], [], []]
    for (q, k, v, do), (weights, inverse, attn), dp in zip(heads, found, dprob):
        dots = jnp.sum(do * attn, axis=0, keepdims=True)
        dscore = (weights.astype(F32) * (dp - dots)).astype(BF16)
        outs[0].append(dot(k, dscore, NN) * (inverse * SCALE))
        outs[1].append(dot((q * inverse).astype(BF16), dscore, NT) * SCALE)
        outs[2].append(dot((do * inverse).astype(BF16), weights, NT))
        outs[3].append(attn)
    return jnp.concatenate([one for pair in outs for one in pair], axis=0)


def ends_of(length_ref):
    lengths = length_ref[...].astype(F32)
    at = lax.broadcasted_iota(jnp.int32, (IMAGES, IMAGES), 0)
    of = lax.broadcasted_iota(jnp.int32, (IMAGES, IMAGES), 1)
    ends = jnp.sum(jnp.where(of <= at, lengths, 0.0), axis=1, keepdims=True)
    starts = jnp.sum(jnp.where(of < at, lengths, 0.0), axis=1, keepdims=True)
    return starts, ends


def marks_of(starts, ends, first, last, size):
    positions = (first + lax.broadcasted_iota(jnp.int32, (1, size), 1)).astype(F32)
    inside = (positions >= starts) & (positions < ends)
    whole = (starts >= first.astype(F32)) & (ends <= last.astype(F32))
    return jnp.where(inside & whole, 1.0, 0.0)


def by_size(rows, step):
    for small, size in zip((0,) + SIZES, SIZES):

        @pl.when((rows > small) & (rows <= size))
        def _():
            step(size)


def inner_kernel(
    place_ref, count_ref, length_ref, mid_ref, grads_ref, attn_ref, frame, total, window, arrived, sent
):
    base = place_ref[0] * SPAN
    columns = [pl.ds(b * ROWS, ROWS) for b in range(GROUP)]
    loads = [
        pltpu.make_async_copy(mid_ref.at[b], frame.at[:, columns[b]], arrived.at[b])
        for b in range(GROUP)
    ]
    for load in loads:
        load.start()

    def scan(i, carry):
        start, n, first = carry
        end = start + count_ref[0, i]
        inside = (start >= base) & (end <= base + SPAN)
        opens = inside & ((n == 0) | (end - first > FILL))
        n = jnp.where(opens, n + 1, n)
        first = jnp.where(opens, start, first)

        @pl.when(inside)
        def _():
            window[0, n - 1] = first
            window[1, n - 1] = end

        return end, n, first

    _, count, _ = lax.fori_loop(0, IMAGES, scan, (jnp.int32(0), jnp.int32(0), jnp.int32(0)))
    frame[:, SPAN:] = jnp.zeros((SLAB, WINDOW), BF16)
    total[...] = jnp.zeros((SLAB, FRAME), BF16)
    starts, ends = ends_of(length_ref)
    for load in loads:
        load.wait()

    def body(n, _):
        first, last = window[0, n], window[1, n]
        offset = first - base
        low = pl.multiple_of(offset // 128 * 128, 128)
        shift = offset - low

        def step(size):
            reach = size + 128
            slab = frame[:, pl.ds(low, reach)].astype(F32)
            slab = pltpu.roll(slab, lax.rem(reach - shift, reach), 1)[:, :size]
            found = attend(slab, marks_of(starts, ends, first, last, size))
            wide = jnp.concatenate([found, jnp.zeros((SLAB, 128), F32)], axis=1)
            wide = pltpu.roll(wide, shift, 1)
            old = total[:, pl.ds(low, reach)].astype(F32)
            total[:, pl.ds(low, reach)] = (old + wide).astype(BF16)

        by_size(last - first, step)
        return 0

    lax.fori_loop(0, count, body, 0)
    stores = [
        pltpu.make_async_copy(total.at[pl.ds(0, GRADS), columns[b]], grads_ref.at[b], sent.at[b])
        for b in range(GROUP)
    ]
    found = total.at[pl.ds(GRADS, PAIR), pl.ds(0, SPAN)]
    stores.append(pltpu.make_async_copy(found, attn_ref, sent.at[GROUP]))
    for store in stores:
        store.start()
    for store in stores:
        store.wait()


RESULT = (
    jax.ShapeDtypeStruct((GROUP, GRADS, ROWS), BF16),
    jax.ShapeDtypeStruct((PAIR, SPAN), BF16),
)


def inner(place, lengths, mid):
    hbm = pl.BlockSpec(memory_space=pl.ANY)
    return pl.pallas_call(
        inner_kernel,
        out_shape=RESULT,
        in_specs=[SCALAR, SCALAR, WHOLE, hbm],
        out_specs=(pl.BlockSpec(memory_space=pltpu.HBM), hbm),
        scratch_shapes=[
            pltpu.VMEM((SLAB, FRAME), BF16),
            pltpu.VMEM((SLAB, FRAME), BF16),
            pltpu.SMEM((2, IMAGES), jnp.int32),
            pltpu.SemaphoreType.DMA((GROUP,)),
            pltpu.SemaphoreType.DMA((GROUP + 1,)),
        ],
        compiler_params=pltpu.CompilerParams(vmem_limit_bytes=VMEM_LIMIT),
        cost_estimate=pl.CostEstimate(flops=20 * 10**9, bytes_accessed=1000, transcendentals=0),
    )(place, lengths, lengths, mid)


def edge_image(place_ref, count_ref, length_ref, mid_ref, left_ref, right_ref, frame, step):
    side = pl.program_id(0)
    border = (place_ref[0] + side) * SPAN

    def scan(i, carry):
        start, first, last = carry
        end = start + count_ref[0, i]
        over = (start < border) & (end > border)
        return end, jnp.where(over, start, first), jnp.where(over, end, last)

    nothing = jnp.int32(-1)
    _, first, last = lax.fori_loop(0, IMAGES, scan, (jnp.int32(0), nothing, nothing))

    @pl.when(last > 0)
    def _():
        def lay(blocks):
            for at, block in enumerate(blocks):
                frame[:, at * ROWS : (at + 1) * ROWS] = block

        @pl.when(side == 0)
        def _():
            lay([left_ref[0], left_ref[1], mid_ref[0], mid_ref[1]])

        @pl.when(side == 1)
        def _():
            lay([mid_ref[0], mid_ref[1], right_ref[0], right_ref[1]])

        starts, ends = ends_of(length_ref)
        offset = first - (border - WINDOW)

        def sized(size):
            slab = pltpu.roll(frame[...].astype(F32), EDGE - offset, 1)[:, :size]
            found = step(slab, marks_of(starts, ends, first, last, size))
            count = found.shape[0]
            wide = jnp.concatenate([found, jnp.zeros((count, EDGE - size), F32)], axis=1)
            frame[:count, :] = pltpu.roll(wide, offset, 1).astype(BF16)

        by_size(last - first, sized)

    @pl.when(last <= 0)
    def _():
        frame[...] = jnp.zeros((SLAB, EDGE), BF16)

    return pl.ds(pl.multiple_of((1 - side) * WINDOW, WINDOW), WINDOW)


def edge_attn_kernel(
    place_ref, count_ref, length_ref, mid_ref, left_ref, right_ref, attn_in, _, attn_ref, frame
):
    def step(slab, marks):
        return jnp.concatenate([attn for _, _, attn in weigh(slab, marks)[1]], axis=0)

    mine = edge_image(place_ref, count_ref, length_ref, mid_ref, left_ref, right_ref, frame, step)
    attn_ref[...] = (attn_in[...].astype(F32) + frame[:PAIR, mine].astype(F32)).astype(BF16)


def edge_grads_kernel(
    place_ref, count_ref, length_ref, mid_ref, left_ref, right_ref, grads_in, _, grads_ref, frame
):
    mine = edge_image(place_ref, count_ref, length_ref, mid_ref, left_ref, right_ref, frame, attend)
    found = frame[:GRADS, mine]
    for at in range(2):
        term = found[:, at * ROWS : (at + 1) * ROWS]
        grads_ref[at] = (grads_in[at].astype(F32) + term.astype(F32)).astype(BF16)


def edge(place, lengths, mid, left, right, inner_part, after):
    ends = lambda rows: pl.BlockSpec((2, rows, ROWS), lambda i: (i * (GROUP // 2 - 1), 0, 0))
    halo = pl.BlockSpec((2, SLAB, ROWS), lambda i: (0, 0, 0))
    kernel, part, flops = edge_grads_kernel, ends(GRADS), 20 * 10**9
    if inner_part.ndim == 2:
        last = SPAN // WINDOW - 1
        kernel, part, flops = edge_attn_kernel, pl.BlockSpec((PAIR, WINDOW), lambda i: (0, i * last)), 1000
    return pl.pallas_call(
        kernel,
        grid=(2,),
        out_shape=jax.ShapeDtypeStruct(inner_part.shape, BF16),
        in_specs=[
            SCALAR, SCALAR, pl.BlockSpec((1, IMAGES), lambda i: (0, 0)), ends(SLAB), halo, halo, part,
            pl.BlockSpec(memory_space=pl.ANY),
        ],
        out_specs=part,
        input_output_aliases={6: 0},
        scratch_shapes=[pltpu.VMEM((SLAB, EDGE), BF16)],
        compiler_params=pltpu.CompilerParams(
            vmem_limit_bytes=VMEM_LIMIT, dimension_semantics=("arbitrary",)
        ),
        cost_estimate=pl.CostEstimate(flops=flops, bytes_accessed=1000, transcendentals=0),
    )(place, lengths, lengths, mid, left, right, inner_part, after)


def unpack_kernel(back_ref, *out_refs):
    for at, out_ref in enumerate(out_refs):
        rows = slice(at * PAIR, (at + 1) * PAIR)
        whole = jnp.concatenate([back_ref[g, rows, :] for g in range(GROUP)], axis=0)
        out_ref[...] = jnp.transpose(whole)


def unpack(back):
    shape = jax.ShapeDtypeStruct((ROWS, WIDTH), BF16)
    return call(unpack_kernel, (shape,) * 3, [WHOLE], [], 1000)(back)


def proj_kernel(at_ref, mine_ref, other_ref, _, *refs):
    rows, outs, (attn, total) = refs[:GROUP], refs[GROUP:-2], refs[-2:]
    first = at_ref[1] == 0
    mine, other = mine_ref[...], other_ref[...]
    attn[:PAIR, :] = jnp.where(first, mine, other)
    attn[PAIR:, :] = jnp.where(first, other, mine)
    found = jnp.zeros((SLAB, 2 * PAIR), F32)
    for k in range(GROUP):
        begin = pl.multiple_of((at_ref[3] ^ k) * ROWS, ROWS)
        found = found + dot(rows[k][...], attn[:, pl.ds(begin, ROWS)], NT)
    total[...] = found
    for k, out_ref in enumerate(outs):
        begin = pl.multiple_of(lax.rem(at_ref[0] + k, 4) * PAIR, PAIR)
        out_ref[...] = total[pl.ds(begin, PAIR), :].astype(out_ref.dtype)


def partial_proj(at, rows, mine, other, token):
    block = lambda dtype: jax.ShapeDtypeStruct((PAIR, 2 * PAIR), dtype)
    shapes = (block(F32),) + (block(BF16),) * 3
    scratch = [pltpu.VMEM((2 * PAIR, SPAN), BF16), pltpu.VMEM((SLAB, 2 * PAIR), F32)]
    specs = [SCALAR] + [WHOLE] * 2 + [pl.BlockSpec(memory_space=pl.ANY)] + [WHOLE] * GROUP
    args = (at, mine, other, token, *rows)
    return call(proj_kernel, shapes, specs, scratch, 1000, ALL_VMEM)(*args)


def select(blocks, at):
    return sum(jnp.where(at == j, block, 0.0) for j, block in enumerate(blocks))


def sum_kernel(*refs):
    refs[4][...] = refs[0][...] + sum(ref[...].astype(F32) for ref in refs[1:4])


def sum_z(terms):
    shape = jax.ShapeDtypeStruct((PAIR, 2 * PAIR), F32)
    return call(sum_kernel, shape, [WHOLE] * 4, [], 1000)(*terms)


def pick_x_kernel(at_ref, one_ref, two_ref, *outs):
    total = one_ref[...] + two_ref[...]
    blocks = [total[j * 36 : (j + 1) * 36] for j in range(4)]
    for k, out_ref in enumerate(outs):
        out_ref[...] = select(blocks, lax.rem(at_ref[2] + k, 4))


def pick_x(at, one, two):
    shape = jax.ShapeDtypeStruct((36, 2 * PAIR), F32)
    return call(pick_x_kernel, (shape,) * 4, [SCALAR] + [WHOLE] * 2, [], 1000)(at, one, two)


def join_x_kernel(at_ref, *refs):
    terms = [ref[...] for ref in refs[:4]]
    for j in range(4):
        block = select(terms, lax.rem(at_ref[2] + 4 - j, 4))
        for y in range(2):
            begin = (4 * y + j) * PAIR
            refs[4][:, begin : begin + PAIR] = block[:, y * PAIR : (y + 1) * PAIR]


def join_x(at, terms):
    shape = jax.ShapeDtypeStruct((36, WIDTH), F32)
    return call(join_x_kernel, shape, [SCALAR] + [WHOLE] * 4, [], 1000)(at, *terms)


def per_device(query, key, value, grad_out, out_proj, lengths):
    seq = lax.axis_index("seq")
    place = jnp.stack([seq // GROUP, (seq // 4) % 2, seq % 4, seq % GROUP])
    count = lax.axis_size("seq")
    within_z = [[GROUP * z + g for g in range(GROUP)] for z in range(4)]

    def shift(block, by):
        return lax.ppermute(block, "seq", [(i, i + by) for i in range(count) if 0 <= i + by < count])

    def corner(block):
        return block[:16, :128]

    def swap(block, axis, by):
        return lax.ppermute(block, axis, [(i, i ^ by) for i in range(lax.axis_size(axis))])

    def exchange(blocks, groups):
        return lax.all_to_all(blocks, "seq", 0, 0, axis_index_groups=groups)

    packed, low, high = pack(query[0], key[0], value[0], grad_out[0], out_proj)
    mid = exchange(packed, within_z)
    first = place[1] == 0
    same = jnp.where(first, low, high)
    near = [same] + [swap(same, "seq", k) for k in range(1, 4)]
    across_y = swap(jnp.where(first, high, low), "seq", 4)
    far = [across_y] + [swap(across_y, "seq", k) for k in range(1, 4)]
    left = shift(mid[GROUP - 2 :], GROUP)
    right = shift(mid[:2], -GROUP)
    grads, attn = inner(place, lengths, mid)
    token = corner(attn) + corner(near[1]) + corner(near[2])
    attn = edge(place, lengths, mid, left, right, attn, token)
    other = swap(attn, "seq", 4)
    grads = edge(place, lengths, mid, left, right, grads, corner(attn))
    token = corner(other) + sum(corner(block) for block in near[3:] + far[1:])
    grads, token = lax.optimization_barrier((grads, token))
    grads = exchange(grads, within_z)
    part, *away = partial_proj(place, near + far, attn, other, token)

    def ahead(block, step, k):
        to = lambda i: i + ((i // step + k) % 4 - i // step % 4) * step
        return lax.ppermute(block, "seq", [(i, to(i)) for i in range(count)])

    part = sum_z([part] + [ahead(b, GROUP, k + 1) for k, b in enumerate(away)])
    part, *away = pick_x(place, part, swap(part, "dp", 1))
    away = [ahead(b, 1, k + 1) for k, b in enumerate(away)]
    grads = unpack(grads)
    grads, away = lax.optimization_barrier((grads, away))
    part = join_x(place, [part] + away)
    part = part + swap(part, "dp", 2)
    return (*(g[None] for g in grads), part)


def solution(mesh):
    rows = P("dp", "seq", None)
    return jax.shard_map(
        per_device,
        mesh=mesh,
        in_specs=(rows, rows, rows, rows, P(), P("dp", None)),
        out_specs=(rows, rows, rows, P("seq", None)),
        check_vma=False,
    )
```

```python
import jax
import jax.numpy as jnp
from jax import lax
from jax.experimental import pallas as pl
from jax.experimental.pallas import tpu as pltpu
from jax.sharding import PartitionSpec as P

HEADS = 16
HEAD_DIM = 72
ROWS = 256
WIDTH = 1152
IMAGES = 32
GROUP = 8
PAIR = 2 * HEAD_DIM
SLAB = 4 * PAIR
GRADS = 3 * PAIR
SPAN = GROUP * ROWS
WINDOW = 512
SIZES = (256, 384, WINDOW)
FRAME = SPAN + WINDOW
EDGE = 2 * WINDOW
SCALE = HEAD_DIM ** (-0.5)
LOG2E = 1.4426950408889634
FAR = 1e30
BF16 = jnp.bfloat16
F32 = jnp.float32
VMEM_LIMIT = 24 * 1024 * 1024
ALL_VMEM = 56 * 1024 * 1024

NN = (((1,), (0,)), ((), ()))
NT = (((1,), (1,)), ((), ()))
TN = (((0,), (0,)), ((), ()))
TNT = (((0,), (1,)), ((), ()))
SCALAR = pl.BlockSpec(memory_space=pltpu.SMEM)
WHOLE = pl.BlockSpec(memory_space=pltpu.VMEM)


def dot(a, b, dims):
    return lax.dot_general(a, b, dims, preferred_element_type=F32)


def call(kernel, out_shape, in_specs, scratch, flops, limit=VMEM_LIMIT):
    return pl.pallas_call(
        kernel,
        out_shape=out_shape,
        in_specs=in_specs,
        out_specs=jax.tree.map(lambda _: WHOLE, out_shape),
        scratch_shapes=scratch,
        compiler_params=pltpu.CompilerParams(vmem_limit_bytes=limit),
        cost_estimate=pl.CostEstimate(flops=flops, bytes_accessed=1000, transcendentals=0),
    )


def pack_kernel(q_ref, k_ref, v_ref, go_ref, proj_ref, out_ref, *halves):
    go = jnp.transpose(go_ref[...])
    for y, half_ref in enumerate(halves):
        for z in range(4):
            half_ref[z * PAIR : (z + 1) * PAIR, :] = go[(2 * z + y) * PAIR : (2 * z + y + 1) * PAIR]
    d_attn = jnp.transpose(dot(go_ref[...], proj_ref[...], NN).astype(BF16))
    turned = [jnp.transpose(ref[...]) for ref in (q_ref, k_ref, v_ref)] + [d_attn]
    for at in range(4):
        for g in range(GROUP):
            out_ref[g, at * PAIR : (at + 1) * PAIR, :] = turned[at][g * PAIR : (g + 1) * PAIR]


def pack(q, k, v, go, proj):
    half = jax.ShapeDtypeStruct((SLAB, ROWS), BF16)
    shapes = (jax.ShapeDtypeStruct((GROUP, SLAB, ROWS), BF16), half, half)
    return call(pack_kernel, shapes, [WHOLE] * 5, [], 1000, ALL_VMEM)(q, k, v, go, proj)


def weigh(slab, marks):
    own = jnp.sum(marks, axis=0, keepdims=True)
    marks = marks.astype(BF16)
    bias = (dot(marks, marks, TN) - 1.0) * FAR
    heads, found = [], []
    for h in range(2):
        q, k, v, do = (
            slab[a * PAIR + h * HEAD_DIM : a * PAIR + (h + 1) * HEAD_DIM] for a in range(4)
        )
        heads.append((q, k.astype(BF16), v.astype(BF16), do * own))
    scores = [dot(k, q.astype(BF16), TN) + bias for q, k, v, do in heads]
    for (q, k, v, do), score in zip(heads, scores):
        top = jnp.max(score, axis=0, keepdims=True)
        weights = jnp.exp2((score - top) * (SCALE * LOG2E))
        inverse = 1.0 / jnp.sum(weights, axis=0, keepdims=True)
        weights = weights.astype(BF16)
        attn = (dot(v, weights, NN) * (inverse * own)).astype(BF16).astype(F32)
        found.append((weights, inverse, attn))
    return heads, found


def attend(slab, marks):
    heads, found = weigh(slab, marks)
    dprob = [dot(v, do.astype(BF16), TN) for q, k, v, do in heads]
    outs = [[], [], [], []]
    for (q, k, v, do), (weights, inverse, attn), dp in zip(heads, found, dprob):
        dots = jnp.sum(do * attn, axis=0, keepdims=True)
        dscore = (weights.astype(F32) * (dp - dots)).astype(BF16)
        outs[0].append(dot(k, dscore, NN) * (inverse * SCALE))
        outs[1].append(dot((q * inverse).astype(BF16), dscore, NT) * SCALE)
        outs[2].append(dot((do * inverse).astype(BF16), weights, NT))
        outs[3].append(attn)
    return jnp.concatenate([one for pair in outs for one in pair], axis=0)


def ends_of(length_ref):
    lengths = length_ref[...].astype(F32)
    at = lax.broadcasted_iota(jnp.int32, (IMAGES, IMAGES), 0)
    of = lax.broadcasted_iota(jnp.int32, (IMAGES, IMAGES), 1)
    ends = jnp.sum(jnp.where(of <= at, lengths, 0.0), axis=1, keepdims=True)
    starts = jnp.sum(jnp.where(of < at, lengths, 0.0), axis=1, keepdims=True)
    return starts, ends


def marks_of(starts, ends, first, last, size):
    positions = (first + lax.broadcasted_iota(jnp.int32, (1, size), 1)).astype(F32)
    inside = (positions >= starts) & (positions < ends)
    whole = (starts >= first.astype(F32)) & (ends <= last.astype(F32))
    return jnp.where(inside & whole, 1.0, 0.0)


def by_size(rows, step):
    for small, size in zip((0,) + SIZES, SIZES):

        @pl.when((rows > small) & (rows <= size))
        def _():
            step(size)


def inner_kernel(
    place_ref, count_ref, length_ref, mid_ref, grads_ref, attn_ref, frame, total, window, arrived, sent
):
    base = place_ref[0] * SPAN
    columns = [pl.ds(b * ROWS, ROWS) for b in range(GROUP)]
    loads = [
        pltpu.make_async_copy(mid_ref.at[b], frame.at[:, columns[b]], arrived.at[b])
        for b in range(GROUP)
    ]
    for load in loads:
        load.start()

    def scan(i, carry):
        start, n, first = carry
        end = start + count_ref[0, i]
        inside = (start >= base) & (end <= base + SPAN)
        short = (start - first <= SIZES[0]) & (end - start <= SIZES[0])
        opens = inside & ((n == 0) | (end - first > jnp.where(short, SIZES[1], WINDOW)))
        n = jnp.where(opens, n + 1, n)
        first = jnp.where(opens, start, first)

        @pl.when(inside)
        def _():
            window[0, n - 1] = first
            window[1, n - 1] = end

        return end, n, first

    _, count, _ = lax.fori_loop(0, IMAGES, scan, (jnp.int32(0), jnp.int32(0), jnp.int32(0)))
    frame[:, SPAN:] = jnp.zeros((SLAB, WINDOW), BF16)
    total[...] = jnp.zeros((SLAB, FRAME), BF16)
    starts, ends = ends_of(length_ref)
    for load in loads:
        load.wait()

    def body(n, _):
        first, last = window[0, n], window[1, n]
        offset = first - base
        low = pl.multiple_of(offset // 128 * 128, 128)
        shift = offset - low

        def step(size):
            reach = size + 128
            slab = frame[:, pl.ds(low, reach)].astype(F32)
            slab = pltpu.roll(slab, lax.rem(reach - shift, reach), 1)[:, :size]
            found = attend(slab, marks_of(starts, ends, first, last, size))
            wide = jnp.concatenate([found, jnp.zeros((SLAB, 128), F32)], axis=1)
            wide = pltpu.roll(wide, shift, 1)
            old = total[:, pl.ds(low, reach)].astype(F32)
            total[:, pl.ds(low, reach)] = (old + wide).astype(BF16)

        by_size(last - first, step)
        return 0

    lax.fori_loop(0, count, body, 0)
    stores = [
        pltpu.make_async_copy(total.at[pl.ds(0, GRADS), columns[b]], grads_ref.at[b], sent.at[b])
        for b in range(GROUP)
    ]
    found = total.at[pl.ds(GRADS, PAIR), pl.ds(0, SPAN)]
    stores.append(pltpu.make_async_copy(found, attn_ref, sent.at[GROUP]))
    for store in stores:
        store.start()
    for store in stores:
        store.wait()


RESULT = (
    jax.ShapeDtypeStruct((GROUP, GRADS, ROWS), BF16),
    jax.ShapeDtypeStruct((PAIR, SPAN), BF16),
)


def inner(place, lengths, mid):
    hbm = pl.BlockSpec(memory_space=pl.ANY)
    return pl.pallas_call(
        inner_kernel,
        out_shape=RESULT,
        in_specs=[SCALAR, SCALAR, WHOLE, hbm],
        out_specs=(pl.BlockSpec(memory_space=pltpu.HBM), hbm),
        scratch_shapes=[
            pltpu.VMEM((SLAB, FRAME), BF16),
            pltpu.VMEM((SLAB, FRAME), BF16),
            pltpu.SMEM((2, IMAGES), jnp.int32),
            pltpu.SemaphoreType.DMA((GROUP,)),
            pltpu.SemaphoreType.DMA((GROUP + 1,)),
        ],
        compiler_params=pltpu.CompilerParams(vmem_limit_bytes=VMEM_LIMIT),
        cost_estimate=pl.CostEstimate(flops=20 * 10**9, bytes_accessed=1000, transcendentals=0),
    )(place, lengths, lengths, mid)


def edge_image(place_ref, count_ref, length_ref, mid_ref, left_ref, right_ref, frame, step):
    side = pl.program_id(0)
    border = (place_ref[0] + side) * SPAN

    def scan(i, carry):
        start, first, last = carry
        end = start + count_ref[0, i]
        over = (start < border) & (end > border)
        return end, jnp.where(over, start, first), jnp.where(over, end, last)

    nothing = jnp.int32(-1)
    _, first, last = lax.fori_loop(0, IMAGES, scan, (jnp.int32(0), nothing, nothing))

    @pl.when(last > 0)
    def _():
        def lay(blocks):
            for at, block in enumerate(blocks):
                frame[:, at * ROWS : (at + 1) * ROWS] = block

        @pl.when(side == 0)
        def _():
            lay([left_ref[0], left_ref[1], mid_ref[0], mid_ref[1]])

        @pl.when(side == 1)
        def _():
            lay([mid_ref[0], mid_ref[1], right_ref[0], right_ref[1]])

        starts, ends = ends_of(length_ref)
        offset = first - (border - WINDOW)

        def sized(size):
            slab = pltpu.roll(frame[...].astype(F32), EDGE - offset, 1)[:, :size]
            found = step(slab, marks_of(starts, ends, first, last, size))
            count = found.shape[0]
            wide = jnp.concatenate([found, jnp.zeros((count, EDGE - size), F32)], axis=1)
            frame[:count, :] = pltpu.roll(wide, offset, 1).astype(BF16)

        by_size(last - first, sized)

    @pl.when(last <= 0)
    def _():
        frame[...] = jnp.zeros((SLAB, EDGE), BF16)

    return pl.ds(pl.multiple_of((1 - side) * WINDOW, WINDOW), WINDOW)


def edge_attn_kernel(
    place_ref, count_ref, length_ref, mid_ref, left_ref, right_ref, attn_in, _, attn_ref, frame
):
    def step(slab, marks):
        return jnp.concatenate([attn for _, _, attn in weigh(slab, marks)[1]], axis=0)

    mine = edge_image(place_ref, count_ref, length_ref, mid_ref, left_ref, right_ref, frame, step)
    attn_ref[...] = (attn_in[...].astype(F32) + frame[:PAIR, mine].astype(F32)).astype(BF16)


def edge_grads_kernel(
    place_ref, count_ref, length_ref, mid_ref, left_ref, right_ref, grads_in, _, grads_ref, frame
):
    mine = edge_image(place_ref, count_ref, length_ref, mid_ref, left_ref, right_ref, frame, attend)
    found = frame[:GRADS, mine]
    for at in range(2):
        term = found[:, at * ROWS : (at + 1) * ROWS]
        grads_ref[at] = (grads_in[at].astype(F32) + term.astype(F32)).astype(BF16)


def edge(place, lengths, mid, left, right, inner_part, after):
    ends = lambda rows: pl.BlockSpec((2, rows, ROWS), lambda i: (i * (GROUP // 2 - 1), 0, 0))
    halo = pl.BlockSpec((2, SLAB, ROWS), lambda i: (0, 0, 0))
    kernel, part, flops = edge_grads_kernel, ends(GRADS), 20 * 10**9
    if inner_part.ndim == 2:
        last = SPAN // WINDOW - 1
        kernel, part, flops = edge_attn_kernel, pl.BlockSpec((PAIR, WINDOW), lambda i: (0, i * last)), 1000
    return pl.pallas_call(
        kernel,
        grid=(2,),
        out_shape=jax.ShapeDtypeStruct(inner_part.shape, BF16),
        in_specs=[
            SCALAR, SCALAR, pl.BlockSpec((1, IMAGES), lambda i: (0, 0)), ends(SLAB), halo, halo, part,
            pl.BlockSpec(memory_space=pl.ANY),
        ],
        out_specs=part,
        input_output_aliases={6: 0},
        scratch_shapes=[pltpu.VMEM((SLAB, EDGE), BF16)],
        compiler_params=pltpu.CompilerParams(
            vmem_limit_bytes=VMEM_LIMIT, dimension_semantics=("arbitrary",)
        ),
        cost_estimate=pl.CostEstimate(flops=flops, bytes_accessed=1000, transcendentals=0),
    )(place, lengths, lengths, mid, left, right, inner_part, after)


def unpack_kernel(back_ref, *out_refs):
    for at, out_ref in enumerate(out_refs):
        rows = slice(at * PAIR, (at + 1) * PAIR)
        whole = jnp.concatenate([back_ref[g, rows, :] for g in range(GROUP)], axis=0)
        out_ref[...] = jnp.transpose(whole)


def unpack(back):
    shape = jax.ShapeDtypeStruct((ROWS, WIDTH), BF16)
    return call(unpack_kernel, (shape,) * 3, [WHOLE], [], 1000)(back)


def proj_kernel(at_ref, mine_ref, other_ref, _, *refs):
    rows, outs, (attn, total) = refs[:GROUP], refs[GROUP:-2], refs[-2:]
    first = at_ref[1] == 0
    mine, other = mine_ref[...], other_ref[...]
    attn[:PAIR, :] = jnp.where(first, mine, other)
    attn[PAIR:, :] = jnp.where(first, other, mine)
    found = jnp.zeros((SLAB, 2 * PAIR), F32)
    for k in range(GROUP):
        begin = pl.multiple_of((at_ref[3] ^ k) * ROWS, ROWS)
        found = found + dot(rows[k][...], attn[:, pl.ds(begin, ROWS)], NT)
    total[...] = found
    for k, out_ref in enumerate(outs):
        begin = pl.multiple_of(lax.rem(at_ref[0] + k, 4) * PAIR, PAIR)
        out_ref[...] = total[pl.ds(begin, PAIR), :].astype(out_ref.dtype)


def partial_proj(at, rows, mine, other, token):
    block = lambda dtype: jax.ShapeDtypeStruct((PAIR, 2 * PAIR), dtype)
    shapes = (block(F32),) + (block(BF16),) * 3
    scratch = [pltpu.VMEM((2 * PAIR, SPAN), BF16), pltpu.VMEM((SLAB, 2 * PAIR), F32)]
    specs = [SCALAR] + [WHOLE] * 2 + [pl.BlockSpec(memory_space=pl.ANY)] + [WHOLE] * GROUP
    args = (at, mine, other, token, *rows)
    return call(proj_kernel, shapes, specs, scratch, 1000, ALL_VMEM)(*args)


def select(blocks, at):
    return sum(jnp.where(at == j, block, 0.0) for j, block in enumerate(blocks))


def sum_kernel(*refs):
    refs[4][...] = refs[0][...] + sum(ref[...].astype(F32) for ref in refs[1:4])


def sum_z(terms):
    shape = jax.ShapeDtypeStruct((PAIR, 2 * PAIR), F32)
    return call(sum_kernel, shape, [WHOLE] * 4, [], 1000)(*terms)


def pick_x_kernel(at_ref, one_ref, two_ref, *outs):
    total = one_ref[...] + two_ref[...]
    blocks = [total[j * 36 : (j + 1) * 36] for j in range(4)]
    for k, out_ref in enumerate(outs):
        out_ref[...] = select(blocks, lax.rem(at_ref[2] + k, 4))


def pick_x(at, one, two):
    shape = jax.ShapeDtypeStruct((36, 2 * PAIR), F32)
    return call(pick_x_kernel, (shape,) * 4, [SCALAR] + [WHOLE] * 2, [], 1000)(at, one, two)


def join_x_kernel(at_ref, *refs):
    terms = [ref[...] for ref in refs[:4]]
    for j in range(4):
        block = select(terms, lax.rem(at_ref[2] + 4 - j, 4))
        for y in range(2):
            begin = (4 * y + j) * PAIR
            refs[4][:, begin : begin + PAIR] = block[:, y * PAIR : (y + 1) * PAIR]


def join_x(at, terms):
    shape = jax.ShapeDtypeStruct((36, WIDTH), F32)
    return call(join_x_kernel, shape, [SCALAR] + [WHOLE] * 4, [], 1000)(at, *terms)


def per_device(query, key, value, grad_out, out_proj, lengths):
    seq = lax.axis_index("seq")
    place = jnp.stack([seq // GROUP, (seq // 4) % 2, seq % 4, seq % GROUP])
    count = lax.axis_size("seq")
    within_z = [[GROUP * z + g for g in range(GROUP)] for z in range(4)]

    def shift(block, by):
        return lax.ppermute(block, "seq", [(i, i + by) for i in range(count) if 0 <= i + by < count])

    def corner(block):
        return block[:16, :128]

    def swap(block, axis, by):
        return lax.ppermute(block, axis, [(i, i ^ by) for i in range(lax.axis_size(axis))])

    def exchange(blocks, groups):
        return lax.all_to_all(blocks, "seq", 0, 0, axis_index_groups=groups)

    packed, low, high = pack(query[0], key[0], value[0], grad_out[0], out_proj)
    mid = exchange(packed, within_z)
    first = place[1] == 0
    same = jnp.where(first, low, high)
    near = [same] + [swap(same, "seq", k) for k in range(1, 4)]
    across_y = swap(jnp.where(first, high, low), "seq", 4)
    far = [across_y] + [swap(across_y, "seq", k) for k in range(1, 4)]
    left = shift(mid[GROUP - 2 :], GROUP)
    right = shift(mid[:2], -GROUP)
    grads, attn = inner(place, lengths, mid)
    token = corner(attn) + corner(near[1]) + corner(near[2])
    attn = edge(place, lengths, mid, left, right, attn, token)
    other = swap(attn, "seq", 4)
    grads = edge(place, lengths, mid, left, right, grads, corner(attn))
    token = corner(other) + sum(corner(block) for block in near[3:] + far[1:])
    grads, token = lax.optimization_barrier((grads, token))
    grads = exchange(grads, within_z)
    part, *away = partial_proj(place, near + far, attn, other, token)

    def ahead(block, step, k):
        to = lambda i: i + ((i // step + k) % 4 - i // step % 4) * step
        return lax.ppermute(block, "seq", [(i, to(i)) for i in range(count)])

    part = sum_z([part] + [ahead(b, GROUP, k + 1) for k, b in enumerate(away)])
    part, *away = pick_x(place, part, swap(part, "dp", 1))
    away = [ahead(b, 1, k + 1) for k, b in enumerate(away)]
    grads = unpack(grads)
    grads, away = lax.optimization_barrier((grads, away))
    part = join_x(place, [part] + away)
    part = part + swap(part, "dp", 2)
    return (*(g[None] for g in grads), part)


def solution(mesh):
    rows = P("dp", "seq", None)
    return jax.shard_map(
        per_device,
        mesh=mesh,
        in_specs=(rows, rows, rows, rows, P(), P("dp", None)),
        out_specs=(rows, rows, rows, P("seq", None)),
        check_vma=False,
    )
```

```python
import jax
import jax.numpy as jnp
from jax import lax
from jax.experimental import pallas as pl
from jax.experimental.pallas import tpu as pltpu
from jax.sharding import PartitionSpec as P

HEADS = 16
HEAD_DIM = 72
ROWS = 256
WIDTH = 1152
IMAGES = 32
GROUP = 8
PAIR = 2 * HEAD_DIM
SLAB = 4 * PAIR
GRADS = 3 * PAIR
SPAN = GROUP * ROWS
WINDOW = 512
SIZES = (256, 384, WINDOW)
FRAME = SPAN + WINDOW
EDGE = 2 * WINDOW
SCALE = HEAD_DIM ** (-0.5)
LOG2E = 1.4426950408889634
FAR = 1e30
BF16 = jnp.bfloat16
F32 = jnp.float32
VMEM_LIMIT = 24 * 1024 * 1024
ALL_VMEM = 56 * 1024 * 1024

NN = (((1,), (0,)), ((), ()))
NT = (((1,), (1,)), ((), ()))
TN = (((0,), (0,)), ((), ()))
TNT = (((0,), (1,)), ((), ()))
SCALAR = pl.BlockSpec(memory_space=pltpu.SMEM)
WHOLE = pl.BlockSpec(memory_space=pltpu.VMEM)


def dot(a, b, dims):
    return lax.dot_general(a, b, dims, preferred_element_type=F32)


def call(kernel, out_shape, in_specs, scratch, flops, limit=VMEM_LIMIT):
    return pl.pallas_call(
        kernel,
        out_shape=out_shape,
        in_specs=in_specs,
        out_specs=jax.tree.map(lambda _: WHOLE, out_shape),
        scratch_shapes=scratch,
        compiler_params=pltpu.CompilerParams(vmem_limit_bytes=limit),
        cost_estimate=pl.CostEstimate(flops=flops, bytes_accessed=1000, transcendentals=0),
    )


def pack_kernel(q_ref, k_ref, v_ref, go_ref, proj_ref, out_ref, *halves):
    go = jnp.transpose(go_ref[...])
    for y, half_ref in enumerate(halves):
        for z in range(4):
            half_ref[z * PAIR : (z + 1) * PAIR, :] = go[(2 * z + y) * PAIR : (2 * z + y + 1) * PAIR]
    d_attn = jnp.transpose(dot(go_ref[...], proj_ref[...], NN).astype(BF16))
    turned = [jnp.transpose(ref[...]) for ref in (q_ref, k_ref, v_ref)] + [d_attn]
    for at in range(4):
        for g in range(GROUP):
            out_ref[g, at * PAIR : (at + 1) * PAIR, :] = turned[at][g * PAIR : (g + 1) * PAIR]


def pack(q, k, v, go, proj):
    half = jax.ShapeDtypeStruct((SLAB, ROWS), BF16)
    shapes = (jax.ShapeDtypeStruct((GROUP, SLAB, ROWS), BF16), half, half)
    return call(pack_kernel, shapes, [WHOLE] * 5, [], 1000, ALL_VMEM)(q, k, v, go, proj)


def weigh(slab, marks):
    own = jnp.sum(marks, axis=0, keepdims=True)
    marks = marks.astype(BF16)
    bias = (dot(marks, marks, TN) - 1.0) * FAR
    heads, found = [], []
    for h in range(2):
        q, k, v, do = (
            slab[a * PAIR + h * HEAD_DIM : a * PAIR + (h + 1) * HEAD_DIM] for a in range(4)
        )
        heads.append((q, k.astype(BF16), v.astype(BF16), do * own))
    scores = [dot(k, q.astype(BF16), TN) + bias for q, k, v, do in heads]
    for (q, k, v, do), score in zip(heads, scores):
        top = jnp.max(score, axis=0, keepdims=True)
        weights = jnp.exp2((score - top) * (SCALE * LOG2E))
        inverse = 1.0 / jnp.sum(weights, axis=0, keepdims=True)
        weights = weights.astype(BF16)
        attn = (dot(v, weights, NN) * (inverse * own)).astype(BF16).astype(F32)
        found.append((weights, inverse, attn))
    return heads, found


def attend(slab, marks):
    heads, found = weigh(slab, marks)
    dprob = [dot(v, do.astype(BF16), TN) for q, k, v, do in heads]
    outs = [[], [], [], []]
    for (q, k, v, do), (weights, inverse, attn), dp in zip(heads, found, dprob):
        dots = jnp.sum(do * attn, axis=0, keepdims=True)
        dscore = (weights.astype(F32) * (dp - dots)).astype(BF16)
        outs[0].append(dot(k, dscore, NN) * (inverse * SCALE))
        outs[1].append(dot((q * inverse).astype(BF16), dscore, NT) * SCALE)
        outs[2].append(dot((do * inverse).astype(BF16), weights, NT))
        outs[3].append(attn)
    return jnp.concatenate([one for pair in outs for one in pair], axis=0)


def ends_of(length_ref):
    lengths = length_ref[...].astype(F32)
    at = lax.broadcasted_iota(jnp.int32, (IMAGES, IMAGES), 0)
    of = lax.broadcasted_iota(jnp.int32, (IMAGES, IMAGES), 1)
    ends = jnp.sum(jnp.where(of <= at, lengths, 0.0), axis=1, keepdims=True)
    starts = jnp.sum(jnp.where(of < at, lengths, 0.0), axis=1, keepdims=True)
    return starts, ends


def marks_of(starts, ends, first, last, size):
    positions = (first + lax.broadcasted_iota(jnp.int32, (1, size), 1)).astype(F32)
    inside = (positions >= starts) & (positions < ends)
    whole = (starts >= first.astype(F32)) & (ends <= last.astype(F32))
    return jnp.where(inside & whole, 1.0, 0.0)


def by_size(rows, step):
    for small, size in zip((0,) + SIZES, SIZES):

        @pl.when((rows > small) & (rows <= size))
        def _():
            step(size)


def inner_kernel(
    place_ref, count_ref, length_ref, mid_ref, grads_ref, attn_ref, frame, total, window, arrived, sent
):
    base = place_ref[0] * SPAN
    columns = [pl.ds(b * ROWS, ROWS) for b in range(GROUP)]
    loads = [
        pltpu.make_async_copy(mid_ref.at[b], frame.at[:, columns[b]], arrived.at[b])
        for b in range(GROUP)
    ]
    for load in loads:
        load.start()

    def scan(i, carry):
        start, n, first = carry
        end = start + count_ref[0, i]
        inside = (start >= base) & (end <= base + SPAN)
        short = (start - first <= SIZES[0]) & (end - start <= SIZES[0])
        opens = inside & ((n == 0) | (end - first > jnp.where(short, SIZES[1], WINDOW)))
        n = jnp.where(opens, n + 1, n)
        first = jnp.where(opens, start, first)

        @pl.when(inside)
        def _():
            window[0, n - 1] = first
            window[1, n - 1] = end

        return end, n, first

    _, count, _ = lax.fori_loop(0, IMAGES, scan, (jnp.int32(0), jnp.int32(0), jnp.int32(0)))
    frame[:, SPAN:] = jnp.zeros((SLAB, WINDOW), BF16)
    total[...] = jnp.zeros((SLAB, FRAME), BF16)
    starts, ends = ends_of(length_ref)
    for load in loads:
        load.wait()

    def body(n, _):
        first, last = window[0, n], window[1, n]
        offset = first - base
        low = pl.multiple_of(offset // 128 * 128, 128)
        shift = offset - low

        def step(size):
            reach = size + 128
            slab = frame[:, pl.ds(low, reach)].astype(F32)
            slab = pltpu.roll(slab, lax.rem(reach - shift, reach), 1)[:, :size]
            found = attend(slab, marks_of(starts, ends, first, last, size))
            wide = jnp.concatenate([found, jnp.zeros((SLAB, 128), F32)], axis=1)
            wide = pltpu.roll(wide, shift, 1)
            old = total[:, pl.ds(low, reach)].astype(F32)
            total[:, pl.ds(low, reach)] = (old + wide).astype(BF16)

        by_size(last - first, step)
        return 0

    lax.fori_loop(0, count, body, 0)
    stores = [
        pltpu.make_async_copy(total.at[pl.ds(0, GRADS), columns[b]], grads_ref.at[b], sent.at[b])
        for b in range(GROUP)
    ]
    found = total.at[pl.ds(GRADS, PAIR), pl.ds(0, SPAN)]
    stores.append(pltpu.make_async_copy(found, attn_ref, sent.at[GROUP]))
    for store in stores:
        store.start()
    for store in stores:
        store.wait()


RESULT = (
    jax.ShapeDtypeStruct((GROUP, GRADS, ROWS), BF16),
    jax.ShapeDtypeStruct((PAIR, SPAN), BF16),
)


def inner(place, lengths, mid):
    hbm = pl.BlockSpec(memory_space=pl.ANY)
    return pl.pallas_call(
        inner_kernel,
        out_shape=RESULT,
        in_specs=[SCALAR, SCALAR, WHOLE, hbm],
        out_specs=(pl.BlockSpec(memory_space=pltpu.HBM), hbm),
        scratch_shapes=[
            pltpu.VMEM((SLAB, FRAME), BF16),
            pltpu.VMEM((SLAB, FRAME), BF16),
            pltpu.SMEM((2, IMAGES), jnp.int32),
            pltpu.SemaphoreType.DMA((GROUP,)),
            pltpu.SemaphoreType.DMA((GROUP + 1,)),
        ],
        compiler_params=pltpu.CompilerParams(vmem_limit_bytes=VMEM_LIMIT),
        cost_estimate=pl.CostEstimate(flops=20 * 10**9, bytes_accessed=1000, transcendentals=0),
    )(place, lengths, lengths, mid)


def edge_image(place_ref, count_ref, length_ref, mid_ref, left_ref, right_ref, frame, step):
    side = pl.program_id(0)
    border = (place_ref[0] + side) * SPAN

    def scan(i, carry):
        start, first, last = carry
        end = start + count_ref[0, i]
        over = (start < border) & (end > border)
        return end, jnp.where(over, start, first), jnp.where(over, end, last)

    nothing = jnp.int32(-1)
    _, first, last = lax.fori_loop(0, IMAGES, scan, (jnp.int32(0), nothing, nothing))

    @pl.when(last > 0)
    def _():
        def lay(blocks):
            for at, block in enumerate(blocks):
                frame[:, at * ROWS : (at + 1) * ROWS] = block

        @pl.when(side == 0)
        def _():
            lay([left_ref[0], left_ref[1], mid_ref[0], mid_ref[1]])

        @pl.when(side == 1)
        def _():
            lay([mid_ref[0], mid_ref[1], right_ref[0], right_ref[1]])

        starts, ends = ends_of(length_ref)
        offset = first - (border - WINDOW)

        def sized(size):
            slab = pltpu.roll(frame[...].astype(F32), EDGE - offset, 1)[:, :size]
            found = step(slab, marks_of(starts, ends, first, last, size))
            count = found.shape[0]
            wide = jnp.concatenate([found, jnp.zeros((count, EDGE - size), F32)], axis=1)
            frame[:count, :] = pltpu.roll(wide, offset, 1).astype(BF16)

        by_size(last - first, sized)

    @pl.when(last <= 0)
    def _():
        frame[...] = jnp.zeros((SLAB, EDGE), BF16)

    return pl.ds(pl.multiple_of((1 - side) * WINDOW, WINDOW), WINDOW)


def edge_attn_kernel(
    place_ref, count_ref, length_ref, mid_ref, left_ref, right_ref, attn_in, _, attn_ref, frame
):
    def step(slab, marks):
        return jnp.concatenate([attn for _, _, attn in weigh(slab, marks)[1]], axis=0)

    mine = edge_image(place_ref, count_ref, length_ref, mid_ref, left_ref, right_ref, frame, step)
    attn_ref[...] = (attn_in[...].astype(F32) + frame[:PAIR, mine].astype(F32)).astype(BF16)


def edge_grads_kernel(
    place_ref, count_ref, length_ref, mid_ref, left_ref, right_ref, grads_in, _, grads_ref, frame
):
    mine = edge_image(place_ref, count_ref, length_ref, mid_ref, left_ref, right_ref, frame, attend)
    found = frame[:GRADS, mine]
    for at in range(2):
        term = found[:, at * ROWS : (at + 1) * ROWS]
        grads_ref[at] = (grads_in[at].astype(F32) + term.astype(F32)).astype(BF16)


def edge(place, lengths, mid, left, right, inner_part, after):
    ends = lambda rows: pl.BlockSpec((2, rows, ROWS), lambda i: (i * (GROUP // 2 - 1), 0, 0))
    halo = pl.BlockSpec((2, SLAB, ROWS), lambda i: (0, 0, 0))
    kernel, part, flops = edge_grads_kernel, ends(GRADS), 20 * 10**9
    if inner_part.ndim == 2:
        last = SPAN // WINDOW - 1
        kernel, part, flops = edge_attn_kernel, pl.BlockSpec((PAIR, WINDOW), lambda i: (0, i * last)), 1000
    return pl.pallas_call(
        kernel,
        grid=(2,),
        out_shape=jax.ShapeDtypeStruct(inner_part.shape, BF16),
        in_specs=[
            SCALAR, SCALAR, pl.BlockSpec((1, IMAGES), lambda i: (0, 0)), ends(SLAB), halo, halo, part,
            pl.BlockSpec(memory_space=pl.ANY),
        ],
        out_specs=part,
        input_output_aliases={6: 0},
        scratch_shapes=[pltpu.VMEM((SLAB, EDGE), BF16)],
        compiler_params=pltpu.CompilerParams(
            vmem_limit_bytes=VMEM_LIMIT, dimension_semantics=("arbitrary",)
        ),
        cost_estimate=pl.CostEstimate(flops=flops, bytes_accessed=1000, transcendentals=0),
    )(place, lengths, lengths, mid, left, right, inner_part, after)


def unpack_kernel(back_ref, *out_refs):
    for at, out_ref in enumerate(out_refs):
        rows = slice(at * PAIR, (at + 1) * PAIR)
        whole = jnp.concatenate([back_ref[g, rows, :] for g in range(GROUP)], axis=0)
        out_ref[...] = jnp.transpose(whole)


def unpack(back):
    shape = jax.ShapeDtypeStruct((ROWS, WIDTH), BF16)
    return call(unpack_kernel, (shape,) * 3, [WHOLE], [], 1000)(back)


def proj_kernel(at_ref, mine_ref, other_ref, _, *refs):
    rows, outs, (attn, total) = refs[:GROUP], refs[GROUP:-2], refs[-2:]
    first = at_ref[1] == 0
    mine, other = mine_ref[...], other_ref[...]
    attn[:PAIR, :] = jnp.where(first, mine, other)
    attn[PAIR:, :] = jnp.where(first, other, mine)
    found = jnp.zeros((SLAB, 2 * PAIR), F32)
    for k in range(GROUP):
        begin = pl.multiple_of((at_ref[3] ^ k) * ROWS, ROWS)
        found = found + dot(rows[k][...], attn[:, pl.ds(begin, ROWS)], NT)
    total[...] = found
    for k, out_ref in enumerate(outs):
        begin = pl.multiple_of(lax.rem(at_ref[0] + k, 4) * PAIR, PAIR)
        out_ref[...] = total[pl.ds(begin, PAIR), :].astype(out_ref.dtype)


def partial_proj(at, rows, mine, other, token):
    block = lambda dtype: jax.ShapeDtypeStruct((PAIR, 2 * PAIR), dtype)
    shapes = (block(F32),) + (block(BF16),) * 3
    scratch = [pltpu.VMEM((2 * PAIR, SPAN), BF16), pltpu.VMEM((SLAB, 2 * PAIR), F32)]
    specs = [SCALAR] + [WHOLE] * 2 + [pl.BlockSpec(memory_space=pl.ANY)] + [WHOLE] * GROUP
    args = (at, mine, other, token, *rows)
    return call(proj_kernel, shapes, specs, scratch, 1000, ALL_VMEM)(*args)


def select(blocks, at):
    return sum(jnp.where(at == j, block, 0.0) for j, block in enumerate(blocks))


def sum_kernel(*refs):
    refs[4][...] = refs[0][...] + sum(ref[...].astype(F32) for ref in refs[1:4])


def sum_z(terms):
    shape = jax.ShapeDtypeStruct((PAIR, 2 * PAIR), F32)
    return call(sum_kernel, shape, [WHOLE] * 4, [], 1000)(*terms)


def pick_x_kernel(at_ref, one_ref, two_ref, *outs):
    total = one_ref[...] + two_ref[...]
    blocks = [total[j * 36 : (j + 1) * 36] for j in range(4)]
    for k, out_ref in enumerate(outs):
        out_ref[...] = select(blocks, lax.rem(at_ref[2] + k, 4))


def pick_x(at, one, two):
    shape = jax.ShapeDtypeStruct((36, 2 * PAIR), F32)
    return call(pick_x_kernel, (shape,) * 4, [SCALAR] + [WHOLE] * 2, [], 1000)(at, one, two)


def join_x_kernel(at_ref, *refs):
    terms, out_ref, joined = [ref[...] for ref in refs[:4]], refs[4], refs[5]
    for j in range(4):
        block = select(terms, lax.rem(at_ref[2] + 4 - j, 4))
        for y in range(2):
            begin = (4 * y + j) * PAIR
            joined[:, begin : begin + PAIR] = block[:, y * PAIR : (y + 1) * PAIR]
    out_ref[...] = joined[...].astype(BF16)


def join_x(at, terms):
    shape = jax.ShapeDtypeStruct((36, WIDTH), BF16)
    scratch = [pltpu.VMEM((36, WIDTH), F32)]
    return call(join_x_kernel, shape, [SCALAR] + [WHOLE] * 4, scratch, 1000)(at, *terms)


def per_device(query, key, value, grad_out, out_proj, lengths):
    seq = lax.axis_index("seq")
    place = jnp.stack([seq // GROUP, (seq // 4) % 2, seq % 4, seq % GROUP])
    count = lax.axis_size("seq")
    within_z = [[GROUP * z + g for g in range(GROUP)] for z in range(4)]

    def shift(block, by):
        return lax.ppermute(block, "seq", [(i, i + by) for i in range(count) if 0 <= i + by < count])

    def corner(block):
        return block[:16, :128]

    def swap(block, axis, by):
        return lax.ppermute(block, axis, [(i, i ^ by) for i in range(lax.axis_size(axis))])

    def exchange(blocks, groups):
        return lax.all_to_all(blocks, "seq", 0, 0, axis_index_groups=groups)

    packed, low, high = pack(query[0], key[0], value[0], grad_out[0], out_proj)
    mid = exchange(packed, within_z)
    first = place[1] == 0
    same = jnp.where(first, low, high)
    near = [same] + [swap(same, "seq", k) for k in range(1, 4)]
    across_y = swap(jnp.where(first, high, low), "seq", 4)
    far = [across_y] + [swap(across_y, "seq", k) for k in range(1, 4)]
    left = shift(mid[GROUP - 2 :], GROUP)
    right = shift(mid[:2], -GROUP)
    grads, attn = inner(place, lengths, mid)
    token = corner(attn) + corner(near[1]) + corner(near[2])
    attn = edge(place, lengths, mid, left, right, attn, token)
    other = swap(attn, "seq", 4)
    grads = edge(place, lengths, mid, left, right, grads, corner(attn))
    token = corner(other) + sum(corner(block) for block in near[3:] + far[1:])
    grads, token = lax.optimization_barrier((grads, token))
    grads = exchange(grads, within_z)
    part, *away = partial_proj(place, near + far, attn, other, token)

    def ahead(block, step, k):
        to = lambda i: i + ((i // step + k) % 4 - i // step % 4) * step
        return lax.ppermute(block, "seq", [(i, to(i)) for i in range(count)])

    part = sum_z([part] + [ahead(b, GROUP, k + 1) for k, b in enumerate(away)])
    part, *away = pick_x(place, part, swap(part, "dp", 1))
    away = [ahead(b, 1, k + 1) for k, b in enumerate(away)]
    grads = unpack(grads)
    grads, away = lax.optimization_barrier((grads, away))
    part = join_x(place, [part] + away)
    part = part.astype(F32) + swap(part, "dp", 2).astype(F32)
    return (*(g[None] for g in grads), part)


def solution(mesh):
    rows = P("dp", "seq", None)
    return jax.shard_map(
        per_device,
        mesh=mesh,
        in_specs=(rows, rows, rows, rows, P(), P("dp", None)),
        out_specs=(rows, rows, rows, P("seq", None)),
        check_vma=False,
    )
```

```python
import jax
import jax.numpy as jnp
from jax import lax
from jax.experimental import pallas as pl
from jax.experimental.pallas import tpu as pltpu
from jax.sharding import PartitionSpec as P

HEADS = 16
HEAD_DIM = 72
ROWS = 256
WIDTH = 1152
IMAGES = 32
GROUP = 8
PAIR = 2 * HEAD_DIM
SLAB = 4 * PAIR
GRADS = 3 * PAIR
SPAN = GROUP * ROWS
WINDOW = 512
SIZES = (256, 384, WINDOW)
FRAME = SPAN + WINDOW
EDGE = 2 * WINDOW
SCALE = HEAD_DIM ** (-0.5)
LOG2E = 1.4426950408889634
FAR = 1e30
BF16 = jnp.bfloat16
F32 = jnp.float32
VMEM_LIMIT = 24 * 1024 * 1024
ALL_VMEM = 56 * 1024 * 1024

NN = (((1,), (0,)), ((), ()))
NT = (((1,), (1,)), ((), ()))
TN = (((0,), (0,)), ((), ()))
TNT = (((0,), (1,)), ((), ()))
SCALAR = pl.BlockSpec(memory_space=pltpu.SMEM)
WHOLE = pl.BlockSpec(memory_space=pltpu.VMEM)


def dot(a, b, dims):
    return lax.dot_general(a, b, dims, preferred_element_type=F32)


def call(kernel, out_shape, in_specs, scratch, flops, limit=VMEM_LIMIT):
    return pl.pallas_call(
        kernel,
        out_shape=out_shape,
        in_specs=in_specs,
        out_specs=jax.tree.map(lambda _: WHOLE, out_shape),
        scratch_shapes=scratch,
        compiler_params=pltpu.CompilerParams(vmem_limit_bytes=limit),
        cost_estimate=pl.CostEstimate(flops=flops, bytes_accessed=1000, transcendentals=0),
    )


def pack_kernel(q_ref, k_ref, v_ref, go_ref, proj_ref, out_ref, *halves):
    go = jnp.transpose(go_ref[...])
    for y, half_ref in enumerate(halves):
        for z in range(4):
            half_ref[z * PAIR : (z + 1) * PAIR, :] = go[(2 * z + y) * PAIR : (2 * z + y + 1) * PAIR]
    d_attn = jnp.transpose(dot(go_ref[...], proj_ref[...], NN).astype(BF16))
    turned = [jnp.transpose(ref[...]) for ref in (q_ref, k_ref, v_ref)] + [d_attn]
    for at in range(4):
        for g in range(GROUP):
            out_ref[g, at * PAIR : (at + 1) * PAIR, :] = turned[at][g * PAIR : (g + 1) * PAIR]


def pack(q, k, v, go, proj):
    half = jax.ShapeDtypeStruct((SLAB, ROWS), BF16)
    shapes = (jax.ShapeDtypeStruct((GROUP, SLAB, ROWS), BF16), half, half)
    return call(pack_kernel, shapes, [WHOLE] * 5, [], 1000, ALL_VMEM)(q, k, v, go, proj)


def weigh(slab, marks):
    own = jnp.sum(marks, axis=0, keepdims=True)
    marks = marks.astype(BF16)
    bias = (dot(marks, marks, TN) - 1.0) * FAR
    heads, found = [], []
    for h in range(2):
        q, k, v, do = (
            slab[a * PAIR + h * HEAD_DIM : a * PAIR + (h + 1) * HEAD_DIM] for a in range(4)
        )
        heads.append((q, k.astype(BF16), v.astype(BF16), do * own))
    scores = [dot(k, q.astype(BF16), TN) + bias for q, k, v, do in heads]
    for (q, k, v, do), score in zip(heads, scores):
        top = jnp.max(score, axis=0, keepdims=True)
        weights = jnp.exp2((score - top) * (SCALE * LOG2E))
        inverse = 1.0 / jnp.sum(weights, axis=0, keepdims=True)
        weights = weights.astype(BF16)
        attn = (dot(v, weights, NN) * (inverse * own)).astype(BF16).astype(F32)
        found.append((weights, inverse, attn))
    return heads, found


def attend(slab, marks):
    heads, found = weigh(slab, marks)
    dprob = [dot(v, do.astype(BF16), TN) for q, k, v, do in heads]
    outs = [[], [], [], []]
    for (q, k, v, do), (weights, inverse, attn), dp in zip(heads, found, dprob):
        dots = jnp.sum(do * attn, axis=0, keepdims=True)
        dscore = (weights.astype(F32) * (dp - dots)).astype(BF16)
        outs[0].append(dot(k, dscore, NN) * (inverse * SCALE))
        outs[1].append(dot((q * inverse).astype(BF16), dscore, NT) * SCALE)
        outs[2].append(dot((do * inverse).astype(BF16), weights, NT))
        outs[3].append(attn)
    return jnp.concatenate([one for pair in outs for one in pair], axis=0)


def ends_of(length_ref):
    lengths = length_ref[...].astype(F32)
    at = lax.broadcasted_iota(jnp.int32, (IMAGES, IMAGES), 0)
    of = lax.broadcasted_iota(jnp.int32, (IMAGES, IMAGES), 1)
    ends = jnp.sum(jnp.where(of <= at, lengths, 0.0), axis=1, keepdims=True)
    starts = jnp.sum(jnp.where(of < at, lengths, 0.0), axis=1, keepdims=True)
    return starts, ends


def marks_of(starts, ends, first, last, size):
    positions = (first + lax.broadcasted_iota(jnp.int32, (1, size), 1)).astype(F32)
    inside = (positions >= starts) & (positions < ends)
    whole = (starts >= first.astype(F32)) & (ends <= last.astype(F32))
    return jnp.where(inside & whole, 1.0, 0.0)


def by_size(rows, step):
    for small, size in zip((0,) + SIZES, SIZES):

        @pl.when((rows > small) & (rows <= size))
        def _():
            step(size)


def inner_kernel(
    place_ref, count_ref, length_ref, mid_ref, grads_ref, attn_ref, frame, total, window, arrived, sent
):
    base = place_ref[0] * SPAN
    columns = [pl.ds(b * ROWS, ROWS) for b in range(GROUP)]
    loads = [
        pltpu.make_async_copy(mid_ref.at[b], frame.at[:, columns[b]], arrived.at[b])
        for b in range(GROUP)
    ]
    for load in loads:
        load.start()

    def scan(i, carry):
        start, n, first = carry
        end = start + count_ref[0, i]
        inside = (start >= base) & (end <= base + SPAN)
        short = (start - first <= SIZES[0]) & (end - start <= SIZES[0])
        opens = inside & ((n == 0) | (end - first > jnp.where(short, SIZES[1], WINDOW)))
        n = jnp.where(opens, n + 1, n)
        first = jnp.where(opens, start, first)

        @pl.when(inside)
        def _():
            window[0, n - 1] = first
            window[1, n - 1] = end

        return end, n, first

    _, count, _ = lax.fori_loop(0, IMAGES, scan, (jnp.int32(0), jnp.int32(0), jnp.int32(0)))
    frame[:, SPAN:] = jnp.zeros((SLAB, WINDOW), BF16)
    total[...] = jnp.zeros((SLAB, FRAME), BF16)
    starts, ends = ends_of(length_ref)
    for load in loads:
        load.wait()

    def body(n, _):
        first, last = window[0, n], window[1, n]
        offset = first - base
        low = pl.multiple_of(offset // 128 * 128, 128)
        shift = offset - low

        def step(size):
            reach = size + 128
            slab = frame[:, pl.ds(low, reach)].astype(F32)
            slab = pltpu.roll(slab, lax.rem(reach - shift, reach), 1)[:, :size]
            found = attend(slab, marks_of(starts, ends, first, last, size))
            wide = jnp.concatenate([found, jnp.zeros((SLAB, 128), F32)], axis=1)
            wide = pltpu.roll(wide, shift, 1)
            old = total[:, pl.ds(low, reach)].astype(F32)
            total[:, pl.ds(low, reach)] = (old + wide).astype(BF16)

        by_size(last - first, step)
        return 0

    lax.fori_loop(0, count, body, 0)
    stores = [
        pltpu.make_async_copy(total.at[pl.ds(0, GRADS), columns[b]], grads_ref.at[b], sent.at[b])
        for b in range(GROUP)
    ]
    found = total.at[pl.ds(GRADS, PAIR), pl.ds(0, SPAN)]
    stores.append(pltpu.make_async_copy(found, attn_ref, sent.at[GROUP]))
    for store in stores:
        store.start()
    for store in stores:
        store.wait()


RESULT = (
    jax.ShapeDtypeStruct((GROUP, GRADS, ROWS), BF16),
    jax.ShapeDtypeStruct((PAIR, SPAN), BF16),
)


def inner(place, lengths, mid):
    hbm = pl.BlockSpec(memory_space=pl.ANY)
    return pl.pallas_call(
        inner_kernel,
        out_shape=RESULT,
        in_specs=[SCALAR, SCALAR, WHOLE, hbm],
        out_specs=(pl.BlockSpec(memory_space=pltpu.HBM), hbm),
        scratch_shapes=[
            pltpu.VMEM((SLAB, FRAME), BF16),
            pltpu.VMEM((SLAB, FRAME), BF16),
            pltpu.SMEM((2, IMAGES), jnp.int32),
            pltpu.SemaphoreType.DMA((GROUP,)),
            pltpu.SemaphoreType.DMA((GROUP + 1,)),
        ],
        compiler_params=pltpu.CompilerParams(vmem_limit_bytes=VMEM_LIMIT),
        cost_estimate=pl.CostEstimate(flops=20 * 10**9, bytes_accessed=1000, transcendentals=0),
    )(place, lengths, lengths, mid)


def edge_image(place_ref, count_ref, length_ref, mid_ref, left_ref, right_ref, frame, step):
    side = pl.program_id(0)
    border = (place_ref[0] + side) * SPAN

    def scan(i, carry):
        start, first, last = carry
        end = start + count_ref[0, i]
        over = (start < border) & (end > border)
        return end, jnp.where(over, start, first), jnp.where(over, end, last)

    nothing = jnp.int32(-1)
    _, first, last = lax.fori_loop(0, IMAGES, scan, (jnp.int32(0), nothing, nothing))

    @pl.when(last > 0)
    def _():
        def lay(blocks):
            for at, block in enumerate(blocks):
                frame[:, at * ROWS : (at + 1) * ROWS] = block

        @pl.when(side == 0)
        def _():
            lay([left_ref[0], left_ref[1], mid_ref[0], mid_ref[1]])

        @pl.when(side == 1)
        def _():
            lay([mid_ref[0], mid_ref[1], right_ref[0], right_ref[1]])

        starts, ends = ends_of(length_ref)
        offset = first - (border - WINDOW)

        def sized(size):
            slab = pltpu.roll(frame[...].astype(F32), EDGE - offset, 1)[:, :size]
            found = step(slab, marks_of(starts, ends, first, last, size))
            count = found.shape[0]
            wide = jnp.concatenate([found, jnp.zeros((count, EDGE - size), F32)], axis=1)
            frame[:count, :] = pltpu.roll(wide, offset, 1).astype(BF16)

        by_size(last - first, sized)

    @pl.when(last <= 0)
    def _():
        frame[...] = jnp.zeros((SLAB, EDGE), BF16)

    return pl.ds(pl.multiple_of((1 - side) * WINDOW, WINDOW), WINDOW)


def edge_attn_kernel(
    place_ref, count_ref, length_ref, mid_ref, left_ref, right_ref, attn_in, _, attn_ref, frame
):
    def step(slab, marks):
        return jnp.concatenate([attn for _, _, attn in weigh(slab, marks)[1]], axis=0)

    mine = edge_image(place_ref, count_ref, length_ref, mid_ref, left_ref, right_ref, frame, step)
    attn_ref[...] = (attn_in[...].astype(F32) + frame[:PAIR, mine].astype(F32)).astype(BF16)


def edge_grads_kernel(
    place_ref, count_ref, length_ref, mid_ref, left_ref, right_ref, grads_in, _, grads_ref, frame
):
    mine = edge_image(place_ref, count_ref, length_ref, mid_ref, left_ref, right_ref, frame, attend)
    found = frame[:GRADS, mine]
    for at in range(2):
        term = found[:, at * ROWS : (at + 1) * ROWS]
        grads_ref[at] = (grads_in[at].astype(F32) + term.astype(F32)).astype(BF16)


def edge(place, lengths, mid, left, right, inner_part, after):
    ends = lambda rows: pl.BlockSpec((2, rows, ROWS), lambda i: (i * (GROUP // 2 - 1), 0, 0))
    halo = pl.BlockSpec((2, SLAB, ROWS), lambda i: (0, 0, 0))
    kernel, part, flops = edge_grads_kernel, ends(GRADS), 20 * 10**9
    if inner_part.ndim == 2:
        last = SPAN // WINDOW - 1
        kernel, part, flops = edge_attn_kernel, pl.BlockSpec((PAIR, WINDOW), lambda i: (0, i * last)), 1000
    return pl.pallas_call(
        kernel,
        grid=(2,),
        out_shape=jax.ShapeDtypeStruct(inner_part.shape, BF16),
        in_specs=[
            SCALAR, SCALAR, pl.BlockSpec((1, IMAGES), lambda i: (0, 0)), ends(SLAB), halo, halo, part,
            pl.BlockSpec(memory_space=pl.ANY),
        ],
        out_specs=part,
        input_output_aliases={6: 0},
        scratch_shapes=[pltpu.VMEM((SLAB, EDGE), BF16)],
        compiler_params=pltpu.CompilerParams(
            vmem_limit_bytes=VMEM_LIMIT, dimension_semantics=("arbitrary",)
        ),
        cost_estimate=pl.CostEstimate(flops=flops, bytes_accessed=1000, transcendentals=0),
    )(place, lengths, lengths, mid, left, right, inner_part, after)


def unpack_kernel(back_ref, *out_refs):
    for at, out_ref in enumerate(out_refs):
        rows = slice(at * PAIR, (at + 1) * PAIR)
        whole = jnp.concatenate([back_ref[g, rows, :] for g in range(GROUP)], axis=0)
        out_ref[...] = jnp.transpose(whole)


def unpack(back):
    shape = jax.ShapeDtypeStruct((ROWS, WIDTH), BF16)
    return call(unpack_kernel, (shape,) * 3, [WHOLE], [], 1000)(back)


def proj_kernel(at_ref, mine_ref, other_ref, _, *refs):
    rows, outs, (attn, total) = refs[:GROUP], refs[GROUP:-2], refs[-2:]
    first = at_ref[1] == 0
    mine, other = mine_ref[...], other_ref[...]
    attn[:PAIR, :] = jnp.where(first, mine, other)
    attn[PAIR:, :] = jnp.where(first, other, mine)
    found = jnp.zeros((SLAB, 2 * PAIR), F32)
    for k in range(GROUP):
        begin = pl.multiple_of((at_ref[3] ^ k) * ROWS, ROWS)
        found = found + dot(rows[k][...], attn[:, pl.ds(begin, ROWS)], NT)
    total[...] = found
    for k, out_ref in enumerate(outs):
        begin = pl.multiple_of(lax.rem(at_ref[0] + k, 4) * PAIR, PAIR)
        out_ref[...] = total[pl.ds(begin, PAIR), :].astype(out_ref.dtype)


def partial_proj(at, rows, mine, other, token):
    block = lambda dtype: jax.ShapeDtypeStruct((PAIR, 2 * PAIR), dtype)
    shapes = (block(F32),) + (block(BF16),) * 3
    scratch = [pltpu.VMEM((2 * PAIR, SPAN), BF16), pltpu.VMEM((SLAB, 2 * PAIR), F32)]
    specs = [SCALAR] + [WHOLE] * 2 + [pl.BlockSpec(memory_space=pl.ANY)] + [WHOLE] * GROUP
    args = (at, mine, other, token, *rows)
    return call(proj_kernel, shapes, specs, scratch, 1000, ALL_VMEM)(*args)


def select(blocks, at):
    return sum(jnp.where(at == j, block, 0.0) for j, block in enumerate(blocks))


def sum_kernel(*refs):
    total = refs[0][...] + sum(ref[...].astype(F32) for ref in refs[1:4])
    refs[4][...] = total.astype(BF16)


def sum_z(terms):
    shape = jax.ShapeDtypeStruct((PAIR, 2 * PAIR), BF16)
    return call(sum_kernel, shape, [WHOLE] * 4, [], 1000)(*terms)


def pick_x_kernel(at_ref, one_ref, two_ref, *outs):
    total = one_ref[...].astype(F32) + two_ref[...].astype(F32)
    blocks = [total[j * 36 : (j + 1) * 36] for j in range(4)]
    for k, out_ref in enumerate(outs):
        out_ref[...] = select(blocks, lax.rem(at_ref[2] + k, 4))


def pick_x(at, one, two):
    shape = jax.ShapeDtypeStruct((36, 2 * PAIR), F32)
    return call(pick_x_kernel, (shape,) * 4, [SCALAR] + [WHOLE] * 2, [], 1000)(at, one, two)


def join_x_kernel(at_ref, *refs):
    terms, out_ref, joined = [ref[...] for ref in refs[:4]], refs[4], refs[5]
    for j in range(4):
        block = select(terms, lax.rem(at_ref[2] + 4 - j, 4))
        for y in range(2):
            begin = (4 * y + j) * PAIR
            joined[:, begin : begin + PAIR] = block[:, y * PAIR : (y + 1) * PAIR]
    out_ref[...] = joined[...].astype(BF16)


def join_x(at, terms):
    shape = jax.ShapeDtypeStruct((36, WIDTH), BF16)
    scratch = [pltpu.VMEM((36, WIDTH), F32)]
    return call(join_x_kernel, shape, [SCALAR] + [WHOLE] * 4, scratch, 1000)(at, *terms)


def per_device(query, key, value, grad_out, out_proj, lengths):
    seq = lax.axis_index("seq")
    place = jnp.stack([seq // GROUP, (seq // 4) % 2, seq % 4, seq % GROUP])
    count = lax.axis_size("seq")
    within_z = [[GROUP * z + g for g in range(GROUP)] for z in range(4)]

    def shift(block, by):
        return lax.ppermute(block, "seq", [(i, i + by) for i in range(count) if 0 <= i + by < count])

    def corner(block):
        return block[:16, :128]

    def swap(block, axis, by):
        return lax.ppermute(block, axis, [(i, i ^ by) for i in range(lax.axis_size(axis))])

    def exchange(blocks, groups):
        return lax.all_to_all(blocks, "seq", 0, 0, axis_index_groups=groups)

    packed, low, high = pack(query[0], key[0], value[0], grad_out[0], out_proj)
    mid = exchange(packed, within_z)
    first = place[1] == 0
    same = jnp.where(first, low, high)
    near = [same] + [swap(same, "seq", k) for k in range(1, 4)]
    across_y = swap(jnp.where(first, high, low), "seq", 4)
    far = [across_y] + [swap(across_y, "seq", k) for k in range(1, 4)]
    left = shift(mid[GROUP - 2 :], GROUP)
    right = shift(mid[:2], -GROUP)
    grads, attn = inner(place, lengths, mid)
    token = corner(attn) + corner(near[1]) + corner(near[2])
    attn = edge(place, lengths, mid, left, right, attn, token)
    other = swap(attn, "seq", 4)
    grads = edge(place, lengths, mid, left, right, grads, corner(attn))
    token = corner(other) + sum(corner(block) for block in near[3:] + far[1:])
    grads, token = lax.optimization_barrier((grads, token))
    grads = exchange(grads, within_z)
    part, *away = partial_proj(place, near + far, attn, other, token)

    def ahead(block, step, k):
        to = lambda i: i + ((i // step + k) % 4 - i // step % 4) * step
        return lax.ppermute(block, "seq", [(i, to(i)) for i in range(count)])

    part = sum_z([part] + [ahead(b, GROUP, k + 1) for k, b in enumerate(away)])
    part, *away = pick_x(place, part, swap(part, "dp", 1))
    away = [ahead(b, 1, k + 1) for k, b in enumerate(away)]
    grads = unpack(grads)
    grads, away = lax.optimization_barrier((grads, away))
    part = join_x(place, [part] + away)
    part = part.astype(F32) + swap(part, "dp", 2).astype(F32)
    return (*(g[None] for g in grads), part)


def solution(mesh):
    rows = P("dp", "seq", None)
    return jax.shard_map(
        per_device,
        mesh=mesh,
        in_specs=(rows, rows, rows, rows, P(), P("dp", None)),
        out_specs=(rows, rows, rows, P("seq", None)),
        check_vma=False,
    )
```
